512 devices in a mesh: row: 32 (over z, core), col: 16 (over x, y).
Axes of the slice: x: 4, y: 4, z: 16, core: 2. Of those that a mesh axis runs over, the one named last changes fastest.
Arguments:
- grad: bfloat16 [9, 7168, 2048], P(None, 'row', 'col'), may hold values from -600 to 600
- momentum: float32 [9, 7168, 2048], P(None, 'row', 'col'), may hold values from -6 to 6
- trailing_coefficients: float32 [9, 2048, 64], P(None, 'col'), may hold values from -0.125 to 0.125
Outputs:
- update: bfloat16 [9, 7168, 2048], P(None, 'row', 'col')
- momentum_next: float32 [9, 7168, 2048], P(None, 'row', 'col')
- right_factor_upcoming: float32 [9, 2048, 64], P(None, 'col')
The draws below stay inside these ranges and needn't reach their ends.
All inputs are finite; a program needn't handle non-finite values.
Results may differ from the reference program's by a relative error of at most 0.0024.
Values sent between devices are 32-bit elements; how exact they have to be, the bound alone decides.
No kernel may reach another device: no remote copies, remote signals or barrier semaphores. Data moves between devices by JAX's collectives and lax.ppermute only.
A program may use at most 64 MiB of HBM per device.

```python
import math
import jax
import jax.numpy as jnp
from jax import lax

ROWS = 7168
COLS = 2048
RANK = 64
MATS = 9


def draw_grad(key, part):
    key = jax.random.fold_in(key, 11)
    first, second, third = jax.random.split(key, 3)
    rough_rows = jnp.exp(jax.random.uniform(first, (MATS, ROWS, 1), jnp.float32) * math.log(10.0))
    rough_cols = jnp.exp(jax.random.uniform(second, (MATS, 1, COLS), jnp.float32) * math.log(10.0))
    increment_lines = jnp.exp(jnp.arange(ROWS, dtype=jnp.float32) / ROWS * math.log(3.0)).reshape(1, ROWS, 1)
    rise_cols = jnp.exp(jnp.arange(COLS, dtype=jnp.float32) / COLS * math.log(3.0)).reshape(1, 1, COLS)
    base = jax.random.normal(third, (MATS, ROWS, COLS), jnp.float32)
    base = jnp.clip(base, -6.0, 6.0)
    numeric_entries = 0.1 * base * rough_rows * rough_cols * increment_lines * rise_cols
    return numeric_entries.astype(jnp.bfloat16)


def level_of(rng, shape, cuts, least, high):
    factor_of = 1.0
    for position, blocks in cuts:
        steps = jax.random.uniform(jax.random.fold_in(jax.random.fold_in(rng, 6), position), (blocks,), jnp.float32, least / len(cuts), high / len(cuts))
        factor_of = factor_of * jnp.repeat(jnp.exp(steps), shape[position] // blocks).reshape((-1,) + (1,) * (len(shape) - 1 - position))
    return factor_of


def centred(key, extent, deviation, most, pieces=(), kind=jnp.bfloat16):
    values = deviation * jax.random.normal(key, extent, jnp.float32)
    if pieces:
        values = values * level_of(key, extent, pieces, -0.22, 0.18)
    return jnp.clip(values, -most, most).astype(kind)


def setup_inputs(seed: int = 0) -> dict:
    seeds = jax.random.split(jax.random.key(seed), 4)
    return {
        "grad": draw_grad(jax.random.fold_in(seeds[3], 71), 0),
        "momentum": centred(seeds[1], (MATS, ROWS, COLS), 1.0, 6.0, ((1, 32), (2, 16)), jnp.float32),
        "trailing_coefficients": centred(seeds[2], (MATS, COLS, RANK), COLS ** -0.5, 0.125, ((1, 16),), jnp.float32),
    }


retention_coefficient = 0.95
norm_epsilon = 1e-08

def reference(grad, momentum, trailing_coefficients):
    finest_accuracy_setting = lax.Precision.HIGHEST
    blending_velocity = momentum + grad.astype(jnp.float32)
    compressed_velocity = jnp.einsum('ulv,uvw->ulw', blending_velocity, trailing_coefficients, precision=finest_accuracy_setting)
    reduced_gram_matrix = jnp.einsum('dub,duk->dbk', compressed_velocity, compressed_velocity, precision=finest_accuracy_setting)
    lower_factor = jnp.linalg.cholesky(reduced_gram_matrix)
    solved = jax.scipy.linalg.solve_triangular(lower_factor, jnp.swapaxes(compressed_velocity, 1, 2), lower=True)
    orthonormal_basis = jnp.swapaxes(solved, 1, 2)
    cross_product_matrix = jnp.einsum('nws,nwp->nsp', blending_velocity, orthonormal_basis, precision=finest_accuracy_setting)
    column_norm = jnp.sqrt(lax.optimization_barrier(jnp.sum(cross_product_matrix * cross_product_matrix, axis=1, keepdims=True)))
    right_factor_upcoming = cross_product_matrix / (column_norm + norm_epsilon)
    reduced_rank_update = jnp.einsum('fpn,fvn->fpv', orthonormal_basis, cross_product_matrix, precision=finest_accuracy_setting)
    momentum_next = blending_velocity - (1.0 - retention_coefficient) * reduced_rank_update
    update_scale_ratio = math.sqrt(ROWS * COLS / RANK)
    update = (update_scale_ratio * jnp.einsum('fpn,fvn->fpv', orthonormal_basis, right_factor_upcoming, precision=finest_accuracy_setting)).astype(jnp.bfloat16)
    return (update, momentum_next, right_factor_upcoming)
```

```python
import functools
import math

import jax
import jax.numpy as jnp
from jax import lax
from jax.experimental import pallas as pl
from jax.experimental.pallas import tpu as pltpu
from jax.sharding import PartitionSpec as P

DECAY = 1.0 - 0.95
EPS = 1e-08
HIGH = lax.Precision.HIGHEST
F32 = jnp.float32


def dot(a, b, ca=1, cb=0):
    return lax.dot_general(
        a, b, (((ca,), (cb,)), ((), ())), precision=HIGH, preferred_element_type=F32
    )


def blend(g_ref, m_ref, i):
    return m_ref[i] + g_ref[i].astype(F32)


def project_kernel(g_ref, m_ref, v_ref, p_ref):
    mats, rows, _ = m_ref.shape
    half = rows // 2
    for i in range(mats):
        b = blend(g_ref, m_ref, i)
        v = v_ref[i]
        p = dot(b, v)
        p_ref[pl.ds(i * half, half), :] = jnp.concatenate([p[:half], p[half:]], axis=1)


def sum_kernel(x_ref, o_ref):
    total = x_ref[0]
    for i in range(1, x_ref.shape[0]):
        total = total + x_ref[i]
    for i in range(o_ref.shape[0]):
        o_ref[i] = total


def pair_sum_kernel(x_ref, o_ref):
    o_ref[...] = x_ref[0] + x_ref[1]


def products_kernel(g_ref, m_ref, p_ref, o_ref, *, slots):
    mats, rows, _ = m_ref.shape
    half = rows // 2
    rank = 64
    step = rank + rank // 2
    o_ref[...] = jnp.zeros_like(o_ref)
    for i in range(mats):
        b = blend(g_ref, m_ref, i)
        pp = p_ref[pl.ds(i * half, half), :]
        both = jnp.concatenate([b[:half], b[half:], pp], axis=1)
        full = dot(pp, both, 0, 0)
        y = full[:rank, :128] + full[rank:, 128:256]
        gram = full[:rank, 256 : 256 + rank] + full[rank:, 256 + rank :]
        h, s = divmod(i, slots)
        o_ref[h, pl.ds(s * step, rank), :] = y
        o_ref[h, pl.ds(s * step + rank, rank // 2), :] = jnp.concatenate(
            [gram[: rank // 2], gram[rank // 2 :]], axis=1
        )


def factor_kernel(gy_ref, o_ref, *, slots):
    rank = 64
    step = rank + rank // 2
    blocks = rank // 8
    row8 = lax.broadcasted_iota(jnp.int32, (8, 128), 0)
    lane8 = lax.broadcasted_iota(jnp.int32, (8, 128), 1)
    a = []
    for s in range(slots):
        packed = gy_ref[pl.ds(s * step + rank, rank // 2), :]
        gram = jnp.concatenate([packed[:, :rank], packed[:, rank:]], axis=0)
        wide = jnp.concatenate([gram, jnp.zeros_like(gram)], axis=1)
        mine = []
        for q in range(blocks):
            eye = jnp.where(lane8 == row8 + (rank + 8 * q), 1.0, 0.0).astype(F32)
            mine.append(wide[8 * q : 8 * q + 8] + eye)
        a.append(mine)
    for k in range(rank):
        q, r = divmod(k, 8)
        for s in range(slots):
            cols = [
                jnp.broadcast_to(a[s][j][:, k : k + 1], (8, 128)) for j in range(q, blocks)
            ]
            scaled = a[s][q][r : r + 1] / cols[0][r : r + 1]
            scaled = jnp.broadcast_to(scaled, (8, 128))
            for j in range(q, blocks):
                col = cols[j - q]
                if j == q:
                    col = jnp.where(row8 > r, col, 0.0)
                a[s][j] = a[s][j] - col * scaled
    norms = []
    for s in range(slots):
        rows = []
        for q in range(blocks):
            diag = jnp.sum(jnp.where(lane8 == row8 + 8 * q, a[s][q], 0.0), axis=1, keepdims=True)
            rows.append(a[s][q] / jnp.sqrt(diag))
        inv = jnp.concatenate(rows, axis=0)[:, rank:]
        xt = dot(inv, gy_ref[pl.ds(s * step, rank), :])
        n = dot(jnp.ones((8, 128), F32), xt * xt, 1, 1)
        norms.append(n)
        for c in range(o_ref.shape[0]):
            o_ref[c, pl.ds(s * 128, rank), :] = xt
            o_ref[c, pl.ds(s * 128 + rank, rank), :] = jnp.concatenate(
                [inv, jnp.zeros_like(inv)], axis=1
            )
    zero = jnp.zeros((8, rank), F32)
    table = jnp.zeros((8, 128), F32)
    for s in range(slots):
        both = jnp.concatenate([norms[s], zero], axis=1)
        table = jnp.where(row8 == s, both, table)
    for c in range(o_ref.shape[0]):
        o_ref[c, pl.ds(slots * 128, 8), :] = table


def finish_kernel(n_ref, f_ref, g_ref, m_ref, p_ref, u_ref, mo_ref, r_ref, *, slots, scale):
    mats, rows, _ = m_ref.shape
    half = rows // 2
    rank = 64
    total = n_ref[0]
    for i in range(1, n_ref.shape[0]):
        total = total + n_ref[i]
    column = jnp.transpose(total)
    for i in range(mats):
        h, s = divmod(i, slots)
        xt = f_ref[h, pl.ds(s * 128, rank), :]
        inv = f_ref[h, pl.ds(s * 128 + rank, rank), :][:, :rank]
        norm = jnp.sqrt(column[:rank, h * 8 + s : h * 8 + s + 1]) + EPS
        rt = xt / norm
        r_ref[i] = jnp.transpose(rt)
        w = dot(inv, jnp.concatenate([xt, rt], axis=1), 0, 0)
        pp = p_ref[pl.ds(i * half, half), :]
        p = jnp.concatenate([pp[:, :rank], pp[:, rank:]], axis=0)
        out = dot(p, w)
        b = blend(g_ref, m_ref, i)
        mo_ref[i] = b - DECAY * out[:, :128]
        u_ref[i] = (scale * out[:, 128:]).astype(jnp.bfloat16)


def call(kernel, out, *args):
    return pl.pallas_call(
        kernel,
        out_shape=out,
        compiler_params=pltpu.CompilerParams(vmem_limit_bytes=48 * 1024 * 1024),
    )(*args)


def shape(*dims, dtype=F32):
    return jax.ShapeDtypeStruct(dims, dtype)


def on_device(grad, momentum, trailing_coefficients):
    mats, rows, cols = momentum.shape
    rank = trailing_coefficients.shape[2]
    n_col = lax.axis_size("col")
    n_row = lax.axis_size("row")
    n_z = n_row // 2
    along_z = [[2 * z + c for z in range(n_z)] for c in range(2)]
    pairs = [[2 * z, 2 * z + 1] for z in range(n_z)]
    scale = math.sqrt(rows * n_row * cols * n_col / rank)
    slots = 5

    part = call(project_kernel, shape(1024, 128), grad, momentum, trailing_coefficients)
    pieces = lax.all_to_all(part.reshape(n_col, 64, 128), "col", 0, 0)
    summed = call(sum_kernel, shape(n_col, 64, 128), pieces)
    projected = lax.all_to_all(summed, "col", 0, 0).reshape(1024, 128)

    products = call(
        functools.partial(products_kernel, slots=slots), shape(2, 512, 128), grad, momentum, projected
    )
    products = lax.all_to_all(products, "row", 0, 0, axis_index_groups=pairs)
    products = call(pair_sum_kernel, shape(512, 128), products)
    pieces = lax.all_to_all(
        products.reshape(n_z, 32, 128), "row", 0, 0, axis_index_groups=along_z
    )
    summed = call(sum_kernel, shape(n_z, 32, 128), pieces)
    products = lax.all_to_all(summed, "row", 0, 0, axis_index_groups=along_z).reshape(512, 128)

    factors = call(
        functools.partial(factor_kernel, slots=slots), shape(2, slots * 128 + 8, 128), products
    )
    factors = lax.all_to_all(factors, "row", 0, 0, axis_index_groups=pairs)
    squares = factors[:, slots * 128 :, :].reshape(1, 16, 128)
    squares = lax.all_to_all(jnp.broadcast_to(squares, (n_col, 16, 128)), "col", 0, 0)

    return call(
        functools.partial(finish_kernel, slots=slots, scale=scale),
        (
            shape(mats, rows, cols, dtype=jnp.bfloat16),
            shape(mats, rows, cols),
            shape(mats, cols, rank),
        ),
        squares,
        factors,
        grad,
        momentum,
        projected,
    )


def solution(mesh):
    return jax.shard_map(
        on_device,
        mesh=mesh,
        in_specs=(P(None, "row", "col"), P(None, "row", "col"), P(None, "col", None)),
        out_specs=(P(None, "row", "col"), P(None, "row", "col"), P(None, "col", None)),
        check_vma=False,
    )
```

```python
import functools
import math

import jax
import jax.numpy as jnp
from jax import lax
from jax.experimental import pallas as pl
from jax.experimental.pallas import tpu as pltpu
from jax.sharding import PartitionSpec as P

DECAY = 1.0 - 0.95
EPS = 1e-08
HIGH = lax.Precision.HIGHEST
F32 = jnp.float32


def dot(a, b, ca=1, cb=0):
    return lax.dot_general(
        a, b, (((ca,), (cb,)), ((), ())), precision=HIGH, preferred_element_type=F32
    )


def split(x):
    hi = x.astype(jnp.bfloat16)
    return hi, (x - hi.astype(F32)).astype(jnp.bfloat16)


def project_kernel(g_hbm, m_hbm, v_hbm, b_ref, p_ref, g_ref, m_ref, v_ref, sem):
    mats, rows, _ = m_ref.shape
    half = rows // 2
    copies = [
        [
            pltpu.make_async_copy(src.at[i], dst.at[i], sem.at[i, j])
            for j, (src, dst) in enumerate(((m_hbm, m_ref), (g_hbm, g_ref), (v_hbm, v_ref)))
        ]
        for i in range(mats)
    ]
    for some in copies:
        for copy in some:
            copy.start()
    for i in range(mats):
        for copy in copies[i]:
            copy.wait()
        b = m_ref[i] + g_ref[i].astype(F32)
        b_ref[i] = b
        p = dot(b, v_ref[i], 1, 1)
        p_ref[pl.ds(i * half, half), :] = jnp.concatenate([p[:half], p[half:]], axis=1)


def sum_kernel(x_ref, o_ref):
    total = x_ref[0]
    for i in range(1, x_ref.shape[0]):
        total = total + x_ref[i]
    for i in range(o_ref.shape[0]):
        o_ref[i] = total


def pair_sum_kernel(x_ref, y_ref, o_ref):
    o_ref[...] = x_ref[...] + y_ref[...]


def products_kernel(h_ref, b_ref, p_ref, o_ref, *, slots):
    mats, rows, _ = b_ref.shape
    half = rows // 2
    rank = 64
    step = rank + rank // 2
    for s in range(slots):
        i = jnp.minimum(h_ref[0] * slots + s, mats - 1)
        b = b_ref[i]
        pp = p_ref[pl.ds(pl.multiple_of(i * half, 8), half), :]
        both = jnp.concatenate([b[:half], b[half:], pp], axis=1)
        full = dot(pp, both, 0, 0)
        y = full[:rank, :128] + full[rank:, 128:256]
        gram = full[:rank, 256 : 256 + rank] + full[rank:, 256 + rank :]
        o_ref[pl.ds(s * step, rank), :] = y
        o_ref[pl.ds(s * step + rank, rank // 2), :] = jnp.concatenate(
            [gram[: rank // 2], gram[rank // 2 :]], axis=1
        )


def factor_kernel(gy_ref, o_ref, rows_ref, *, slots):
    rank = 64
    step = rank + rank // 2
    lane = lax.broadcasted_iota(jnp.int32, (slots, 128), 1)

    def splat(row, at):
        return jnp.broadcast_to(row[:, at : at + 1], (slots, 128))

    a = []
    for i in range(rank):
        packed = gy_ref[pl.ds(rank + i % 32, slots, stride=step), :]
        if i >= 32:
            packed = pltpu.roll(packed, 64, 1)
        packed = jnp.where(lane < rank, packed, 0.0)
        a.append(jnp.where(lane == rank + i, 1.0, packed))
    size = 8
    for first in range(0, rank, size):
        e = [[splat(a[first + i], first + j) for j in range(i + 1)] for i in range(size)]
        inverse = []
        for p in range(size):
            inverse.append(1.0 / e[p][p])
            low = [None] * size
            for i in range(p + 1, size):
                low[i] = e[i][p] * inverse[p]
            for i in range(p + 1, size):
                for j in range(p + 1, i + 1):
                    e[i][j] = e[i][j] - low[i] * e[j][p]
                a[first + i] = a[first + i] - low[i] * a[first + p]
        scaled = [a[first + p] * inverse[p] for p in range(size)]
        for i in range(first + size, rank):
            terms = [splat(a[first + p], i) * scaled[p] for p in range(size)]
            while len(terms) > 1:
                terms = [terms[t] + terms[t + 1] for t in range(0, len(terms), 2)]
            a[i] = a[i] - terms[0]
        for p in range(size):
            rows_ref[pl.ds(first + p, slots, stride=rank), :] = a[first + p] * lax.rsqrt(e[p][p])
    row8 = lax.broadcasted_iota(jnp.int32, (8, 128), 0)
    table = jnp.zeros((8, 128), F32)
    zero = jnp.zeros((8, rank), F32)
    for s in range(slots):
        inv = rows_ref[pl.ds(s * rank, rank), :][:, rank:]
        xt = dot(inv, gy_ref[pl.ds(s * step, rank), :])
        n = dot(jnp.ones((8, 128), F32), xt * xt, 1, 1)
        table = jnp.where(row8 == s, jnp.concatenate([n, zero], axis=1), table)
        packed = jnp.concatenate([inv[: rank // 2], inv[rank // 2 :]], axis=1)
        for c in range(o_ref.shape[0]):
            o_ref[c, pl.ds(s * step, rank), :] = xt
            o_ref[c, pl.ds(s * step + rank, rank // 2), :] = packed
    for c in range(o_ref.shape[0]):
        o_ref[c, pl.ds(slots * step, 8), :] = table


def finish_kernel(
    n_ref, f_ref, b_ref, p_ref, u_hbm, mo_hbm, r_hbm, u_ref, mo_ref, r_ref, sem, *, slots, scale
):
    mats, rows, _ = b_ref.shape
    half = rows // 2
    rank = 64
    step = rank + rank // 2
    total = n_ref[0]
    for i in range(1, n_ref.shape[0]):
        total = total + n_ref[i]
    column = jnp.transpose(total)
    copies = []
    for i in range(mats):
        h, s = divmod(i, slots)
        xt = f_ref[h, pl.ds(s * step, rank), :]
        packed = f_ref[h, pl.ds(s * step + rank, rank // 2), :]
        inv = jnp.concatenate([packed[:, :rank], packed[:, rank:]], axis=0)
        norm = jnp.sqrt(column[:rank, h * 8 + s : h * 8 + s + 1]) + EPS
        rt = xt / norm
        r_ref[i] = rt
        w = dot(inv, jnp.concatenate([xt, rt], axis=1), 0, 0)
        wh, wl = split(w)
        pp = p_ref[pl.ds(i * half, half), :]
        p = jnp.concatenate([pp[:, :rank], pp[:, rank:]], axis=0)
        ph, pl_ = split(p)
        out = lax.dot_general(
            jnp.concatenate([ph, ph, pl_, pl_], axis=1),
            jnp.concatenate([wh, wl, wh, wl], axis=0),
            (((1,), (0,)), ((), ())),
            preferred_element_type=F32,
        )
        mo_ref[i] = b_ref[i] - DECAY * out[:, :128]
        u_ref[i] = (scale * out[:, 128:]).astype(jnp.bfloat16)
        for j, (src, dst) in enumerate(((u_ref, u_hbm), (mo_ref, mo_hbm), (r_ref, r_hbm))):
            copy = pltpu.make_async_copy(src.at[i], dst.at[i], sem.at[i, j])
            copy.start()
            copies.append(copy)
    for copy in copies:
        copy.wait()


def call(kernel, out, *args, ins=None, outs=None, scratch=(), flops=0, moved=0):
    vmem = pl.BlockSpec(memory_space=pltpu.VMEM)
    several = isinstance(out, tuple)
    outs = outs or ((vmem,) * len(out) if several else vmem)
    return pl.pallas_call(
        kernel,
        out_shape=out,
        in_specs=ins or (vmem,) * len(args),
        out_specs=outs,
        scratch_shapes=scratch,
        cost_estimate=pl.CostEstimate(flops=flops, bytes_accessed=moved, transcendentals=0),
        compiler_params=pltpu.CompilerParams(vmem_limit_bytes=32 * 1024 * 1024),
    )(*args)


def shape(*dims, dtype=F32):
    return jax.ShapeDtypeStruct(dims, dtype)


def on_device(grad, momentum, trailing_coefficients):
    mats, rows, cols = momentum.shape
    rank = trailing_coefficients.shape[2]
    n_col = lax.axis_size("col")
    n_row = lax.axis_size("row")
    core = lax.rem(lax.axis_index("row"), 2)
    near = [[(4 * h + l) * 2 + c for l in range(4)] for h in range(4) for c in range(2)]
    far = [[(4 * h + l) * 2 + c for h in range(4)] for l in range(4) for c in range(2)]
    pairs = [[2 * z, 2 * z + 1] for z in range(n_row // 2)]
    swap = [(i, i ^ 1) for i in range(n_row)]
    scale = math.sqrt(rows * n_row * cols * n_col / rank)
    slots = 5
    step = rank + rank // 2
    hbm = pl.BlockSpec(memory_space=pltpu.HBM)
    vmem = pl.BlockSpec(memory_space=pltpu.VMEM)
    smem = pl.BlockSpec(memory_space=pltpu.SMEM)

    blended, part = call(
        project_kernel,
        (shape(mats, rows, cols), shape(1024, 128)),
        grad,
        momentum,
        jnp.swapaxes(trailing_coefficients, 1, 2),
        ins=(hbm,) * 3,
        scratch=(
            pltpu.VMEM((mats, rows, cols), jnp.bfloat16),
            pltpu.VMEM((mats, rows, cols), F32),
            pltpu.VMEM((mats, rank, cols), F32),
            pltpu.SemaphoreType.DMA((mats, 3)),
        ),
    )
    pieces = lax.all_to_all(part.reshape(n_col, 64, 128), "col", 0, 0)
    summed = call(sum_kernel, shape(n_col, 64, 128), pieces)
    projected = lax.all_to_all(summed, "col", 0, 0).reshape(1024, 128)

    def products(half):
        return call(
            functools.partial(products_kernel, slots=slots),
            shape(slots * step, 128),
            half.reshape(1),
            blended,
            projected,
            ins=(smem, vmem, vmem),
            flops=5 * 10**8,
            moved=2 * 10**6,
        )

    theirs = lax.ppermute(products(1 - core), "row", swap)
    mine = products(core)
    pieces = call(pair_sum_kernel, shape(slots * step, 128), mine, theirs)
    quarter = slots * step // 4
    pieces = lax.all_to_all(
        pieces.reshape(4, quarter, 128), "row", 0, 0, axis_index_groups=near
    )
    summed = call(sum_kernel, shape(4, quarter, 128), pieces)
    pieces = lax.all_to_all(summed, "row", 0, 0, axis_index_groups=far)
    summed = call(sum_kernel, shape(4, quarter, 128), pieces)
    reduced = lax.all_to_all(summed, "row", 0, 0, axis_index_groups=near)

    factors = call(
        functools.partial(factor_kernel, slots=slots),
        shape(2, slots * step + 8, 128),
        reduced.reshape(slots * step, 128),
        scratch=(pltpu.VMEM((slots * rank, 128), F32),),
    )
    factors = lax.all_to_all(factors, "row", 0, 0, axis_index_groups=pairs)
    squares = factors[:, slots * step :, :].reshape(1, 16, 128)
    squares = lax.all_to_all(jnp.broadcast_to(squares, (n_col, 16, 128)), "col", 0, 0)

    update, momentum_next, right = call(
        functools.partial(finish_kernel, slots=slots, scale=scale),
        (
            shape(mats, rows, cols, dtype=jnp.bfloat16),
            shape(mats, rows, cols),
            shape(mats, rank, cols),
        ),
        squares,
        factors,
        blended,
        projected,
        outs=(hbm,) * 3,
        scratch=(
            pltpu.VMEM((mats, rows, cols), jnp.bfloat16),
            pltpu.VMEM((mats, rows, cols), F32),
            pltpu.VMEM((mats, rank, cols), F32),
            pltpu.SemaphoreType.DMA((mats, 3)),
        ),
    )
    return update, momentum_next, jnp.swapaxes(right, 1, 2)


def solution(mesh):
    return jax.shard_map(
        on_device,
        mesh=mesh,
        in_specs=(P(None, "row", "col"), P(None, "row", "col"), P(None, "col", None)),
        out_specs=(P(None, "row", "col"), P(None, "row", "col"), P(None, "col", None)),
        check_vma=False,
    )
```

```python
import functools
import math

import jax
import jax.numpy as jnp
from jax import lax
from jax.experimental import pallas as pl
from jax.experimental.pallas import tpu as pltpu
from jax.sharding import PartitionSpec as P

DECAY = 1.0 - 0.95
EPS = 1e-08
F32 = jnp.float32
BF16 = jnp.bfloat16
ORDER = ((0, 0), (0, 1), (1, 0), (1, 1), (0, 2), (2, 0))


def parts(x, count):
    out = []
    for _ in range(count):
        out.append(x.astype(BF16))
        x = x - out[-1].astype(F32)
    return out


def dot(a, b, ca=1, cb=0, terms=6):
    count = 3 if terms > 4 else 2
    a, b = parts(a, count), parts(b, count)
    return lax.dot_general(
        jnp.concatenate([a[i] for i, _ in ORDER[:terms]], axis=ca),
        jnp.concatenate([b[j] for _, j in ORDER[:terms]], axis=cb),
        (((ca,), (cb,)), ((), ())),
        preferred_element_type=F32,
    )


def project_kernel(b_ref, v_ref, p_ref):
    mats, rows, _ = b_ref.shape
    half = rows // 2
    for i in range(mats):
        p = dot(b_ref[i], v_ref[i], 1, 1, 3)
        p_ref[pl.ds(i * half, half), :] = jnp.concatenate([p[:half], p[half:]], axis=1)


def sum_kernel(x_ref, o_ref):
    total = x_ref[0]
    for i in range(1, x_ref.shape[0]):
        total = total + x_ref[i]
    for i in range(o_ref.shape[0]):
        o_ref[i] = total


def pair_sum_kernel(x_ref, y_ref, o_ref):
    o_ref[...] = x_ref[...] + y_ref[...]


def products_kernel(h_ref, b_ref, p_ref, o_ref, *, slots):
    mats, rows, _ = b_ref.shape
    half = rows // 2
    rank = 64
    step = rank + rank // 2
    for s in range(slots):
        i = jnp.minimum(h_ref[0] * slots + s, mats - 1)
        b = b_ref[i]
        pp = p_ref[pl.ds(pl.multiple_of(i * half, 8), half), :]
        full = dot(pp, jnp.concatenate([b[:half], b[half:], pp], axis=1), 0, 0)
        gram = full[:rank, 256 : 256 + rank] + full[rank:, 256 + rank :]
        o_ref[pl.ds(s * step, rank), :] = full[:rank, :128] + full[rank:, 128:256]
        o_ref[pl.ds(s * step + rank, rank // 2), :] = jnp.concatenate(
            [gram[: rank // 2], gram[rank // 2 :]], axis=1
        )


def factor_kernel(gy_ref, o_ref, a_ref, h_ref, *, slots):
    rank = 64
    size = 16
    step = rank + rank // 2
    row = lax.broadcasted_iota(jnp.int32, (rank, rank), 0)
    lane = lax.broadcasted_iota(jnp.int32, (rank, rank), 1)
    eye = jnp.where(lane == row, 1.0, 0.0).astype(F32)
    for s in range(slots):
        packed = gy_ref[pl.ds(s * step + rank, rank // 2), :]
        gram = jnp.concatenate([packed[:, :rank], packed[:, rank:]], axis=0)
        a_ref[pl.ds(s * rank, rank), :] = jnp.concatenate([gram, eye], axis=1)
    for first in range(0, rank, size):
        a = [a_ref[pl.ds(first + p, slots, stride=rank), :] for p in range(size)]
        e = [
            [
                jnp.broadcast_to(a[i][:, first + j : first + j + 1], (slots, 128))
                for j in range(i + 1)
            ]
            for i in range(size)
        ]
        for p in range(size):
            root = lax.rsqrt(e[p][p])
            root = root * (1.5 - 0.5 * e[p][p] * root * root)
            a[p] = a[p] * root
            low = [None] * size
            for i in range(p + 1, size):
                low[i] = e[i][p] * root
            for i in range(p + 1, size):
                for j in range(p + 1, i + 1):
                    e[i][j] = e[i][j] - low[i] * low[j]
                a[i] = a[i] - low[i] * a[p]
            h_ref[pl.ds(first + p, slots, stride=rank), :] = a[p]
        left = rank - first - size
        if left:
            for s in range(slots):
                h = h_ref[pl.ds(s * rank + first, size), :]
                at = pl.ds(s * rank + first + size, left)
                a_ref[at, :] = a_ref[at, :] - dot(h[:, first + size : rank], h, 0, 0)
    row8 = lax.broadcasted_iota(jnp.int32, (8, 128), 0)
    table = jnp.zeros((8, 128), F32)
    zero = jnp.zeros((8, rank), F32)
    for s in range(slots):
        inv = h_ref[pl.ds(s * rank, rank), :][:, rank:]
        xt = dot(inv, gy_ref[pl.ds(s * step, rank), :])
        squares = dot(jnp.ones((8, 128), F32), xt * xt, 1, 1)
        table = jnp.where(row8 == s, jnp.concatenate([squares, zero], axis=1), table)
        o_ref[pl.ds(s * step, rank), :] = xt
        o_ref[pl.ds(s * step + rank, rank // 2), :] = jnp.concatenate(
            [inv[: rank // 2], inv[rank // 2 :]], axis=1
        )
    o_ref[pl.ds(slots * step, 8), :] = table


def retain_kernel(core_ref, mine_ref, theirs_ref, b_ref, p_ref, mo_ref, q_ref, *, slots):
    mats, rows, _ = b_ref.shape
    half = rows // 2
    rank = 64
    step = rank + rank // 2
    core = core_ref[0]
    for i in range(mats):
        h, s = divmod(i, slots)
        at = pl.ds(s * step, step)
        factor = jnp.where(core == h, mine_ref[at, :], theirs_ref[at, :])
        xt, packed = factor[:rank], factor[rank:]
        inv = jnp.concatenate([packed[:, :rank], packed[:, rank:]], axis=0)
        pp = p_ref[pl.ds(i * half, half), :]
        p = jnp.concatenate([pp[:, :rank], pp[:, rank:]], axis=0)
        qh, ql = parts(dot(p, inv, 1, 1, 4), 2)
        q = jnp.concatenate([qh, qh, ql, ql], axis=1)
        q_ref[i] = q
        xh, xl = parts(xt, 2)
        low_rank = jnp.dot(
            q, jnp.concatenate([xh, xl, xh, xl], axis=0), preferred_element_type=F32
        )
        mo_ref[i] = b_ref[i] - DECAY * low_rank


def update_kernel(
    core_ref, n_ref, mine_ref, theirs_ref, q_ref, u_ref, r_ref, *, slots, scale
):
    mats = q_ref.shape[0]
    rank = 64
    step = rank + rank // 2
    core = core_ref[0]
    total = n_ref[0]
    for i in range(1, n_ref.shape[0]):
        total = total + n_ref[i]
    inverse = 1.0 / (jnp.sqrt(jnp.transpose(total)) + EPS)
    for i in range(mats):
        h, s = divmod(i, slots)
        at = pl.ds(s * step, rank)
        xt = jnp.where(core == h, mine_ref[at, :], theirs_ref[at, :])
        rt = xt * jnp.where(core == h, inverse[:rank, s : s + 1], inverse[:rank, 8 + s : 9 + s])
        r_ref[i] = rt
        rh, rl = parts(scale * rt, 2)
        u_ref[i] = jnp.dot(
            q_ref[i], jnp.concatenate([rh, rl, rh, rl], axis=0), preferred_element_type=F32
        ).astype(BF16)


def call(kernel, out, *args, scalar=False, scratch=(), flops=0, moved=0):
    vmem = pl.BlockSpec(memory_space=pltpu.VMEM)
    first = pl.BlockSpec(memory_space=pltpu.SMEM) if scalar else vmem
    return pl.pallas_call(
        kernel,
        out_shape=out,
        in_specs=(first,) + (vmem,) * (len(args) - 1),
        out_specs=(vmem,) * len(out) if isinstance(out, tuple) else vmem,
        scratch_shapes=scratch,
        cost_estimate=pl.CostEstimate(flops=flops, bytes_accessed=moved, transcendentals=0),
        compiler_params=pltpu.CompilerParams(vmem_limit_bytes=32 * 1024 * 1024),
    )(*args)


def shape(*dims, dtype=F32):
    return jax.ShapeDtypeStruct(dims, dtype)


def on_device(grad, momentum, trailing_coefficients):
    mats, rows, cols = momentum.shape
    rank = trailing_coefficients.shape[2]
    n_col = lax.axis_size("col")
    n_row = lax.axis_size("row")
    core = lax.rem(lax.axis_index("row"), 2)
    here = core.reshape(1)
    near = [[(4 * h + l) * 2 + c for l in range(4)] for h in range(4) for c in range(2)]
    far = [[(4 * h + l) * 2 + c for h in range(4)] for l in range(4) for c in range(2)]
    swap = [(i, i ^ 1) for i in range(n_row)]
    scale = math.sqrt(rows * n_row * cols * n_col / rank)
    slots = 5
    step = rank + rank // 2
    work = dict(flops=5 * 10**8, moved=2 * 10**6)

    blended = momentum + grad.astype(F32)
    part = call(
        project_kernel, shape(1024, 128), blended, jnp.swapaxes(trailing_coefficients, 1, 2)
    )
    pieces = lax.all_to_all(part.reshape(n_col, 64, 128), "col", 0, 0)
    summed = call(sum_kernel, shape(n_col, 64, 128), pieces)
    projected = lax.all_to_all(summed, "col", 0, 0).reshape(1024, 128)

    def products(half):
        return call(
            functools.partial(products_kernel, slots=slots),
            shape(slots * step, 128),
            half,
            blended,
            projected,
            scalar=True,
            **work,
        )

    theirs = lax.ppermute(products(1 - here), "row", swap)
    mine = products(here)
    pieces = call(pair_sum_kernel, shape(slots * step, 128), mine, theirs)
    quarter = slots * step // 4
    pieces = lax.all_to_all(
        pieces.reshape(4, quarter, 128), "row", 0, 0, axis_index_groups=near
    )
    summed = call(sum_kernel, shape(4, quarter, 128), pieces)
    pieces = lax.all_to_all(summed, "row", 0, 0, axis_index_groups=far)
    summed = call(sum_kernel, shape(4, quarter, 128), pieces)
    reduced = lax.all_to_all(summed, "row", 0, 0, axis_index_groups=near)

    mine = call(
        functools.partial(factor_kernel, slots=slots),
        shape(slots * step + 8, 128),
        reduced.reshape(slots * step, 128),
        scratch=(pltpu.VMEM((slots * rank, 128), F32),) * 2,
    )
    theirs = lax.ppermute(mine, "row", swap)
    squares = jnp.concatenate([mine[slots * step :], theirs[slots * step :]], axis=0)
    squares = lax.all_to_all(
        jnp.broadcast_to(squares[None], (n_col, 16, 128)), "col", 0, 0
    )
    momentum_next, orthonormal = call(
        functools.partial(retain_kernel, slots=slots),
        (shape(mats, rows, cols), shape(mats, rows, 4 * rank, dtype=BF16)),
        here,
        mine,
        theirs,
        blended,
        projected,
        scalar=True,
        **work,
    )
    update, right = call(
        functools.partial(update_kernel, slots=slots, scale=scale),
        (shape(mats, rows, cols, dtype=BF16), shape(mats, rank, cols)),
        here,
        squares,
        mine,
        theirs,
        orthonormal,
        scalar=True,
    )
    return update, momentum_next, jnp.swapaxes(right, 1, 2)


def solution(mesh):
    return jax.shard_map(
        on_device,
        mesh=mesh,
        in_specs=(P(None, "row", "col"), P(None, "row", "col"), P(None, "col", None)),
        out_specs=(P(None, "row", "col"), P(None, "row", "col"), P(None, "col", None)),
        check_vma=False,
    )
```

```python
import functools
import math

import jax
import jax.numpy as jnp
from jax import lax
from jax.experimental import pallas as pl
from jax.experimental.pallas import tpu as pltpu
from jax.sharding import PartitionSpec as P

DECAY = 1.0 - 0.95
EPS = 1e-08
F32 = jnp.float32
BF16 = jnp.bfloat16
ORDER = ((0, 0), (0, 1), (1, 0), (1, 1), (0, 2), (2, 0))


def parts(x, count):
    out = []
    for _ in range(count):
        out.append(x.astype(BF16))
        x = x - out[-1].astype(F32)
    return out


def dot(a, b, ca=1, cb=0, terms=6):
    count = 3 if terms > 4 else 2
    a, b = parts(a, count), parts(b, count)
    return lax.dot_general(
        jnp.concatenate([a[i] for i, _ in ORDER[:terms]], axis=ca),
        jnp.concatenate([b[j] for _, j in ORDER[:terms]], axis=cb),
        (((ca,), (cb,)), ((), ())),
        preferred_element_type=F32,
    )


def project_kernel(b_ref, v_ref, p_ref):
    mats, rows, _ = b_ref.shape
    half = rows // 2
    for i in range(mats):
        p = dot(b_ref[i], v_ref[i], 1, 1, 3)
        p_ref[pl.ds(i * half, half), :] = jnp.concatenate([p[:half], p[half:]], axis=1)


def sum_kernel(x_ref, o_ref):
    total = x_ref[0]
    for i in range(1, x_ref.shape[0]):
        total = total + x_ref[i]
    for i in range(o_ref.shape[0]):
        o_ref[i] = total


def pair_sum_kernel(x_ref, y_ref, o_ref):
    o_ref[...] = x_ref[...] + y_ref[...]


RANK = 64
FOUR = 4
SHARED = FOUR * RANK
SQUARES = SHARED + RANK // 2
LAST = SQUARES + 2 * (RANK // 2)
HALF_ROWS = LAST + RANK // 2
INVERSES = SQUARES
NORMS = INVERSES + (FOUR + 1) * (RANK // 2)
FACTOR_ROWS = NORMS + 8


def fold(x):
    return jnp.concatenate([x[: RANK // 2], x[RANK // 2 :]], axis=1)


def unfold(x):
    return jnp.concatenate([x[:, :RANK], x[:, RANK:]], axis=0)


def square_iota():
    row = lax.broadcasted_iota(jnp.int32, (RANK, RANK), 0)
    lane = lax.broadcasted_iota(jnp.int32, (RANK, RANK), 1)
    return row, lane


def products_kernel(h_ref, b_ref, p_ref, o_ref):
    mats, rows, _ = b_ref.shape
    half = rows // 2
    h = h_ref[0]
    row, lane = square_iota()
    grams = []
    for s in range(FOUR + 1):
        i = mats - 1 if s == FOUR else h * FOUR + s
        b = b_ref[i]
        at = i * half if s == FOUR else pl.multiple_of(i * half, 8)
        pp = p_ref[pl.ds(at, half), :]
        full = dot(pp, jnp.concatenate([b[:half], b[half:], pp], axis=1), 0, 0)
        y = full[:RANK, :128] + full[RANK:, 128:256]
        if s == FOUR:
            o_ref[pl.ds(SHARED, RANK // 2), :] = fold(jnp.where(h == 0, y[:, :RANK], y[:, RANK:]))
        else:
            o_ref[pl.ds(s * RANK, RANK), :] = y
        grams.append(full[:RANK, 256 : 256 + RANK] + full[RANK:, 256 + RANK :])
    quarter = RANK // 2
    row32 = lax.broadcasted_iota(jnp.int32, (quarter, quarter), 0)
    extra = jnp.zeros((quarter, quarter), F32)
    for t in range(2):
        lower, upper = grams[2 * t], grams[2 * t + 1]
        o_ref[pl.ds(SQUARES + t * quarter, quarter), :] = fold(jnp.where(lane <= row, lower, upper))
        diag = jnp.sum(jnp.where(lane == row, upper, 0.0), axis=0, keepdims=True)
        extra = jnp.where(row32 == 2 * t, diag[:, :quarter], extra)
        extra = jnp.where(row32 == 2 * t + 1, diag[:, quarter:], extra)
    last = grams[FOUR]
    o_ref[pl.ds(LAST, quarter), :] = jnp.concatenate(
        [last[:quarter, :quarter], last[quarter:], extra], axis=1
    )


def read_grams(gy_ref):
    quarter = RANK // 2
    row, lane = square_iota()
    last = gy_ref[pl.ds(LAST, quarter), :]
    extra = last[:, 3 * quarter :]
    grams = []
    for t in range(2):
        square = unfold(gy_ref[pl.ds(SQUARES + t * quarter, quarter), :])
        other = jnp.transpose(square)
        diag = jnp.concatenate([extra[2 * t : 2 * t + 1], extra[2 * t + 1 : 2 * t + 2]], axis=1)
        grams.append(jnp.where(lane <= row, square, other))
        grams.append(jnp.where(lane == row, diag, jnp.where(lane > row, square, other)))
    bottom = last[:, quarter : 3 * quarter]
    top = jnp.concatenate([last[:, :quarter], jnp.transpose(bottom[:, :quarter])], axis=1)
    grams.append(jnp.concatenate([top, bottom], axis=0))
    return grams


def factor_kernel(gy_ref, o_ref, a_ref, h_ref):
    rank = RANK
    slots = FOUR + 1
    size = 16
    row, lane = square_iota()
    eye = jnp.where(lane == row, 1.0, 0.0).astype(F32)
    for s, gram in enumerate(read_grams(gy_ref)):
        a_ref[pl.ds(s * rank, rank), :] = jnp.concatenate([gram, eye], axis=1)
    for first in range(0, rank, size):
        a = [a_ref[pl.ds(first + p, slots, stride=rank), :] for p in range(size)]
        e = [
            [
                jnp.broadcast_to(a[i][:, first + j : first + j + 1], (slots, 128))
                for j in range(i + 1)
            ]
            for i in range(size)
        ]
        for p in range(size):
            root = lax.rsqrt(e[p][p])
            root = root * (1.5 - 0.5 * e[p][p] * root * root)
            a[p] = a[p] * root
            low = [None] * size
            for i in range(p + 1, size):
                low[i] = e[i][p] * root
            for i in range(p + 1, size):
                for j in range(p + 1, i + 1):
                    e[i][j] = e[i][j] - low[i] * low[j]
                a[i] = a[i] - low[i] * a[p]
            h_ref[pl.ds(first + p, slots, stride=rank), :] = a[p]
        left = rank - first - size
        if left:
            for s in range(slots):
                h = h_ref[pl.ds(s * rank + first, size), :]
                at = pl.ds(s * rank + first + size, left)
                a_ref[at, :] = a_ref[at, :] - dot(h[:, first + size : rank], h, 0, 0)
    row8 = lax.broadcasted_iota(jnp.int32, (8, 128), 0)
    table = jnp.zeros((8, 128), F32)
    zero = jnp.zeros((8, rank), F32)
    for s in range(slots):
        inv = h_ref[pl.ds(s * rank, rank), :][:, rank:]
        if s == FOUR:
            xt = dot(inv, unfold(gy_ref[pl.ds(SHARED, rank // 2), :]))
            o_ref[pl.ds(SHARED, rank // 2), :] = fold(xt)
        else:
            xt = dot(inv, gy_ref[pl.ds(s * rank, rank), :])
            o_ref[pl.ds(s * rank, rank), :] = xt
        squares = dot(jnp.ones((8, xt.shape[1]), F32), xt * xt, 1, 1)
        table = jnp.where(row8 == s, jnp.concatenate([squares, zero], axis=1), table)
        o_ref[pl.ds(INVERSES + s * (rank // 2), rank // 2), :] = fold(inv)
    o_ref[pl.ds(NORMS, 8), :] = table


def repeat_norms_kernel(mine_ref, theirs_ref, o_ref):
    both = jnp.concatenate([mine_ref[pl.ds(NORMS, 8), :], theirs_ref[pl.ds(NORMS, 8), :]], axis=0)
    for c in range(o_ref.shape[0]):
        o_ref[c] = both


def read_crossed(core, i, mine_ref, theirs_ref):
    h, s = divmod(i, FOUR)
    if h < 2:
        at = pl.ds(s * RANK, RANK)
        return jnp.where(core == h, mine_ref[at, :], theirs_ref[at, :])
    at = pl.ds(SHARED, RANK // 2)
    mine, theirs = unfold(mine_ref[at, :]), unfold(theirs_ref[at, :])
    return jnp.concatenate(
        [jnp.where(core == 0, mine, theirs), jnp.where(core == 0, theirs, mine)], axis=1
    )


def retain_kernel(core_ref, mine_ref, theirs_ref, b_ref, p_ref, mo_ref, q_ref):
    mats, rows, _ = b_ref.shape
    half = rows // 2
    core = core_ref[0]
    for i in range(mats):
        h, s = divmod(i, FOUR)
        xt = read_crossed(core, i, mine_ref, theirs_ref)
        if h < 2:
            at = pl.ds(INVERSES + s * (RANK // 2), RANK // 2)
            inv = unfold(jnp.where(core == h, mine_ref[at, :], theirs_ref[at, :]))
        else:
            inv = unfold(mine_ref[pl.ds(INVERSES + FOUR * (RANK // 2), RANK // 2), :])
        p = unfold(p_ref[pl.ds(i * half, half), :])
        qh, ql = parts(dot(p, inv, 1, 1, 4), 2)
        q = jnp.concatenate([qh, qh, ql, ql], axis=1)
        q_ref[i] = q
        xh, xl = parts(xt, 2)
        low_rank = jnp.dot(
            q, jnp.concatenate([xh, xl, xh, xl], axis=0), preferred_element_type=F32
        )
        mo_ref[i] = b_ref[i] - DECAY * low_rank


def update_kernel(core_ref, n_ref, mine_ref, theirs_ref, q_ref, u_ref, r_ref, *, scale):
    mats = q_ref.shape[0]
    core = core_ref[0]
    total = n_ref[0]
    for i in range(1, n_ref.shape[0]):
        total = total + n_ref[i]
    row = lax.broadcasted_iota(jnp.int32, total.shape, 0)
    shared = total[FOUR : FOUR + 1] + total[8 + FOUR : 9 + FOUR]
    total = jnp.where(row == FOUR, shared, total)
    inverse = 1.0 / (jnp.sqrt(jnp.transpose(total)) + EPS)
    for i in range(mats):
        h, s = divmod(i, FOUR)
        xt = read_crossed(core, i, mine_ref, theirs_ref)
        if h < 2:
            norm = jnp.where(core == h, inverse[:RANK, s : s + 1], inverse[:RANK, 8 + s : 9 + s])
        else:
            norm = inverse[:RANK, FOUR : FOUR + 1]
        rt = xt * norm
        r_ref[i] = rt
        rh, rl = parts(scale * rt, 2)
        u_ref[i] = jnp.dot(
            q_ref[i], jnp.concatenate([rh, rl, rh, rl], axis=0), preferred_element_type=F32
        ).astype(BF16)


def call(kernel, out, *args, scalar=False, scratch=(), flops=0, moved=0):
    vmem = pl.BlockSpec(memory_space=pltpu.VMEM)
    first = pl.BlockSpec(memory_space=pltpu.SMEM) if scalar else vmem
    return pl.pallas_call(
        kernel,
        out_shape=out,
        in_specs=(first,) + (vmem,) * (len(args) - 1),
        out_specs=(vmem,) * len(out) if isinstance(out, tuple) else vmem,
        scratch_shapes=scratch,
        cost_estimate=pl.CostEstimate(flops=flops, bytes_accessed=moved, transcendentals=0),
        compiler_params=pltpu.CompilerParams(vmem_limit_bytes=32 * 1024 * 1024),
    )(*args)


def shape(*dims, dtype=F32):
    return jax.ShapeDtypeStruct(dims, dtype)


def on_device(grad, momentum, trailing_coefficients):
    mats, rows, cols = momentum.shape
    rank = trailing_coefficients.shape[2]
    n_col = lax.axis_size("col")
    n_row = lax.axis_size("row")
    core = lax.rem(lax.axis_index("row"), 2)
    here = core.reshape(1)
    near = [[(4 * h + l) * 2 + c for l in range(4)] for h in range(4) for c in range(2)]
    far = [[(4 * h + l) * 2 + c for h in range(4)] for l in range(4) for c in range(2)]
    swap = [(i, i ^ 1) for i in range(n_row)]
    scale = math.sqrt(rows * n_row * cols * n_col / rank)
    work = dict(flops=5 * 10**8, moved=2 * 10**6)

    blended = momentum + grad.astype(F32)
    part = call(
        project_kernel, shape(1024, 128), blended, jnp.swapaxes(trailing_coefficients, 1, 2)
    )
    pieces = lax.all_to_all(part.reshape(n_col, 64, 128), "col", 0, 0)
    summed = call(sum_kernel, shape(n_col, 64, 128), pieces)
    projected = lax.all_to_all(summed, "col", 0, 0).reshape(1024, 128)

    def products(half):
        return call(
            products_kernel,
            shape(HALF_ROWS, 128),
            half,
            blended,
            projected,
            scalar=True,
            **work,
        )

    theirs = lax.ppermute(products(1 - here), "row", swap)
    mine = products(here)
    pieces = call(pair_sum_kernel, shape(HALF_ROWS, 128), mine, theirs)
    quarter = HALF_ROWS // 4
    pieces = lax.all_to_all(
        pieces.reshape(4, quarter, 128), "row", 0, 0, axis_index_groups=near
    )
    summed = call(sum_kernel, shape(4, quarter, 128), pieces)
    pieces = lax.all_to_all(summed, "row", 0, 0, axis_index_groups=far)
    summed = call(sum_kernel, shape(4, quarter, 128), pieces)
    reduced = lax.all_to_all(summed, "row", 0, 0, axis_index_groups=near)

    mine = call(
        factor_kernel,
        shape(FACTOR_ROWS, 128),
        reduced.reshape(HALF_ROWS, 128),
        scratch=(pltpu.VMEM(((FOUR + 1) * rank, 128), F32),) * 2,
    )
    theirs = lax.ppermute(mine, "row", swap)
    squares = call(repeat_norms_kernel, shape(n_col, 16, 128), mine, theirs)
    squares = lax.all_to_all(squares, "col", 0, 0)
    momentum_next, orthonormal = call(
        retain_kernel,
        (shape(mats, rows, cols), shape(mats, rows, 4 * rank, dtype=BF16)),
        here,
        mine,
        theirs,
        blended,
        projected,
        scalar=True,
        **work,
    )
    update, right = call(
        functools.partial(update_kernel, scale=scale),
        (shape(mats, rows, cols, dtype=BF16), shape(mats, rank, cols)),
        here,
        squares,
        mine,
        theirs,
        orthonormal,
        scalar=True,
    )
    return update, momentum_next, jnp.swapaxes(right, 1, 2)


def solution(mesh):
    return jax.shard_map(
        on_device,
        mesh=mesh,
        in_specs=(P(None, "row", "col"), P(None, "row", "col"), P(None, "col", None)),
        out_specs=(P(None, "row", "col"), P(None, "row", "col"), P(None, "col", None)),
        check_vma=False,
    )
```

```python
import functools
import math

import jax
import jax.numpy as jnp
from jax import lax
from jax.experimental import pallas as pl
from jax.experimental.pallas import tpu as pltpu
from jax.sharding import PartitionSpec as P

DECAY = 1.0 - 0.95
EPS = 1e-08
F32 = jnp.float32
BF16 = jnp.bfloat16
ORDER = ((0, 0), (0, 1), (1, 0), (1, 1), (0, 2), (2, 0))


def parts(x, count):
    out = []
    for _ in range(count):
        out.append(x.astype(BF16))
        x = x - out[-1].astype(F32)
    return out


def dot(a, b, ca=1, cb=0, terms=6):
    count = 3 if terms > 4 else 2
    a, b = parts(a, count), parts(b, count)
    return lax.dot_general(
        jnp.concatenate([a[i] for i, _ in ORDER[:terms]], axis=ca),
        jnp.concatenate([b[j] for _, j in ORDER[:terms]], axis=cb),
        (((ca,), (cb,)), ((), ())),
        preferred_element_type=F32,
    )


def project_kernel(b_ref, v_ref, p_ref):
    mats, rows, _ = b_ref.shape
    half = rows // 2
    for i in range(mats):
        p = dot(b_ref[i], v_ref[i], 1, 1, 3)
        p_ref[pl.ds(i * half, half), :] = jnp.concatenate([p[:half], p[half:]], axis=1)


def sum_kernel(x_ref, o_ref):
    total = x_ref[0]
    for i in range(1, x_ref.shape[0]):
        total = total + x_ref[i]
    for i in range(o_ref.shape[0]):
        o_ref[i] = total


def pair_sum_kernel(x_ref, y_ref, o_ref):
    o_ref[...] = x_ref[...] + y_ref[...]


RANK = 64
FOUR = 4
SHARED = FOUR * RANK
SQUARES = SHARED + RANK // 2
LAST = SQUARES + 2 * (RANK // 2)
HALF_ROWS = LAST + RANK // 2
INVERSES = SQUARES
FACTOR_ROWS = INVERSES + (FOUR + 1) * (RANK // 2)


def fold(x):
    return jnp.concatenate([x[: RANK // 2], x[RANK // 2 :]], axis=1)


def unfold(x):
    return jnp.concatenate([x[:, :RANK], x[:, RANK:]], axis=0)


def square_iota():
    row = lax.broadcasted_iota(jnp.int32, (RANK, RANK), 0)
    lane = lax.broadcasted_iota(jnp.int32, (RANK, RANK), 1)
    return row, lane


def products_kernel(h_ref, b_ref, p_ref, o_ref):
    mats, rows, _ = b_ref.shape
    half = rows // 2
    h = h_ref[0]
    row, lane = square_iota()
    grams = []
    for s in range(FOUR + 1):
        i = mats - 1 if s == FOUR else h * FOUR + s
        b = b_ref[i]
        at = i * half if s == FOUR else pl.multiple_of(i * half, 8)
        pp = p_ref[pl.ds(at, half), :]
        full = dot(pp, jnp.concatenate([b[:half], b[half:], pp], axis=1), 0, 0)
        y = full[:RANK, :128] + full[RANK:, 128:256]
        if s == FOUR:
            o_ref[pl.ds(SHARED, RANK // 2), :] = fold(jnp.where(h == 0, y[:, :RANK], y[:, RANK:]))
        else:
            o_ref[pl.ds(s * RANK, RANK), :] = y
        grams.append(full[:RANK, 256 : 256 + RANK] + full[RANK:, 256 + RANK :])
    quarter = RANK // 2
    row32 = lax.broadcasted_iota(jnp.int32, (quarter, quarter), 0)
    extra = jnp.zeros((quarter, quarter), F32)
    for t in range(2):
        lower, upper = grams[2 * t], grams[2 * t + 1]
        o_ref[pl.ds(SQUARES + t * quarter, quarter), :] = fold(jnp.where(lane <= row, lower, upper))
        diag = jnp.sum(jnp.where(lane == row, upper, 0.0), axis=0, keepdims=True)
        extra = jnp.where(row32 == 2 * t, diag[:, :quarter], extra)
        extra = jnp.where(row32 == 2 * t + 1, diag[:, quarter:], extra)
    last = grams[FOUR]
    o_ref[pl.ds(LAST, quarter), :] = jnp.concatenate(
        [last[:quarter, :quarter], last[quarter:], extra], axis=1
    )


def read_grams(gy_ref):
    quarter = RANK // 2
    row, lane = square_iota()
    last = gy_ref[pl.ds(LAST, quarter), :]
    extra = last[:, 3 * quarter :]
    grams = []
    for t in range(2):
        square = unfold(gy_ref[pl.ds(SQUARES + t * quarter, quarter), :])
        other = jnp.transpose(square)
        diag = jnp.concatenate([extra[2 * t : 2 * t + 1], extra[2 * t + 1 : 2 * t + 2]], axis=1)
        grams.append(jnp.where(lane <= row, square, other))
        grams.append(jnp.where(lane == row, diag, jnp.where(lane > row, square, other)))
    bottom = last[:, quarter : 3 * quarter]
    top = jnp.concatenate([last[:, :quarter], jnp.transpose(bottom[:, :quarter])], axis=1)
    grams.append(jnp.concatenate([top, bottom], axis=0))
    return grams


def factor_kernel(gy_ref, o_ref, n_ref, a_ref, h_ref):
    rank = RANK
    slots = FOUR + 1
    size = 16
    row, lane = square_iota()
    eye = jnp.where(lane == row, 1.0, 0.0).astype(F32)
    for s, gram in enumerate(read_grams(gy_ref)):
        a_ref[pl.ds(s * rank, rank), :] = jnp.concatenate([gram, eye], axis=1)
    for first in range(0, rank, size):
        a = [a_ref[pl.ds(first + p, slots, stride=rank), :] for p in range(size)]
        e = [
            [
                jnp.broadcast_to(a[i][:, first + j : first + j + 1], (slots, 128))
                for j in range(i + 1)
            ]
            for i in range(size)
        ]
        for p in range(size):
            root = lax.rsqrt(e[p][p])
            a[p] = a[p] * root
            low = [None] * size
            for i in range(p + 1, size):
                low[i] = e[i][p] * root
            for i in range(p + 1, size):
                for j in range(p + 1, i + 1):
                    e[i][j] = e[i][j] - low[i] * low[j]
                a[i] = a[i] - low[i] * a[p]
            h_ref[pl.ds(first + p, slots, stride=rank), :] = a[p]
        left = rank - first - size
        if left:
            for s in range(slots):
                h = h_ref[pl.ds(s * rank + first, size), :]
                at = pl.ds(s * rank + first + size, left)
                a_ref[at, :] = a_ref[at, :] - dot(h[:, first + size : rank], h, 0, 0)
    row8 = lax.broadcasted_iota(jnp.int32, (8, 128), 0)
    table = jnp.zeros((8, 128), F32)
    zero = jnp.zeros((8, rank), F32)
    for s in range(slots):
        inv = h_ref[pl.ds(s * rank, rank), :][:, rank:]
        if s == FOUR:
            xt = dot(inv, unfold(gy_ref[pl.ds(SHARED, rank // 2), :]))
            o_ref[pl.ds(SHARED, rank // 2), :] = fold(xt)
        else:
            xt = dot(inv, gy_ref[pl.ds(s * rank, rank), :])
            o_ref[pl.ds(s * rank, rank), :] = xt
        squares = dot(jnp.ones((8, xt.shape[1]), F32), xt * xt, 1, 1)
        table = jnp.where(row8 == s, jnp.concatenate([squares, zero], axis=1), table)
        o_ref[pl.ds(INVERSES + s * (rank // 2), rank // 2), :] = fold(inv)
    for c in range(n_ref.shape[0]):
        n_ref[c] = table


def read_crossed(core, i, mine_ref, theirs_ref):
    h, s = divmod(i, FOUR)
    if h < 2:
        at = pl.ds(s * RANK, RANK)
        return jnp.where(core == h, mine_ref[at, :], theirs_ref[at, :])
    at = pl.ds(SHARED, RANK // 2)
    mine, theirs = unfold(mine_ref[at, :]), unfold(theirs_ref[at, :])
    return jnp.concatenate(
        [jnp.where(core == 0, mine, theirs), jnp.where(core == 0, theirs, mine)], axis=1
    )


def retain_kernel(core_ref, mine_ref, theirs_ref, b_ref, p_ref, mo_ref, q_ref):
    mats, rows, _ = b_ref.shape
    half = rows // 2
    core = core_ref[0]
    for i in range(mats):
        h, s = divmod(i, FOUR)
        xt = read_crossed(core, i, mine_ref, theirs_ref)
        if h < 2:
            at = pl.ds(INVERSES + s * (RANK // 2), RANK // 2)
            inv = unfold(jnp.where(core == h, mine_ref[at, :], theirs_ref[at, :]))
        else:
            inv = unfold(mine_ref[pl.ds(INVERSES + FOUR * (RANK // 2), RANK // 2), :])
        p = unfold(p_ref[pl.ds(i * half, half), :])
        qh, ql = parts(dot(p, inv, 1, 1, 4), 2)
        q = jnp.concatenate([qh, qh, ql, ql], axis=1)
        q_ref[i] = q
        xh, xl = parts(xt, 2)
        low_rank = jnp.dot(
            q, jnp.concatenate([xh, xl, xh, xl], axis=0), preferred_element_type=F32
        )
        mo_ref[i] = b_ref[i] - DECAY * low_rank


def update_kernel(core_ref, n_ref, mine_ref, theirs_ref, q_ref, u_ref, r_ref, *, scale):
    mats = q_ref.shape[0]
    core = core_ref[0]
    totals = [n_ref[0], n_ref[1]]
    for i in range(2, n_ref.shape[0]):
        totals[i % 2] = totals[i % 2] + n_ref[i]
    row = lax.broadcasted_iota(jnp.int32, totals[0].shape, 0)
    totals[0] = jnp.where(row == FOUR, totals[0] + totals[1], totals[0])
    total = jnp.concatenate(totals, axis=0)
    inverse = 1.0 / (jnp.sqrt(jnp.transpose(total)) + EPS)
    for i in range(mats):
        h, s = divmod(i, FOUR)
        xt = read_crossed(core, i, mine_ref, theirs_ref)
        at = 8 * h + s if h < 2 else FOUR
        rt = xt * inverse[:RANK, at : at + 1]
        r_ref[i] = rt
        rh, rl = parts(scale * rt, 2)
        u_ref[i] = jnp.dot(
            q_ref[i], jnp.concatenate([rh, rl, rh, rl], axis=0), preferred_element_type=F32
        ).astype(BF16)


def call(kernel, out, *args, scalar=False, scratch=(), flops=0, moved=0):
    vmem = pl.BlockSpec(memory_space=pltpu.VMEM)
    first = pl.BlockSpec(memory_space=pltpu.SMEM) if scalar else vmem
    return pl.pallas_call(
        kernel,
        out_shape=out,
        in_specs=(first,) + (vmem,) * (len(args) - 1),
        out_specs=(vmem,) * len(out) if isinstance(out, tuple) else vmem,
        scratch_shapes=scratch,
        cost_estimate=pl.CostEstimate(flops=flops, bytes_accessed=moved, transcendentals=0),
        compiler_params=pltpu.CompilerParams(vmem_limit_bytes=32 * 1024 * 1024),
    )(*args)


def shape(*dims, dtype=F32):
    return jax.ShapeDtypeStruct(dims, dtype)


def on_device(grad, momentum, trailing_coefficients):
    mats, rows, cols = momentum.shape
    rank = trailing_coefficients.shape[2]
    n_col = lax.axis_size("col")
    n_row = lax.axis_size("row")
    core = lax.rem(lax.axis_index("row"), 2)
    near = [[(4 * h + l) * 2 + c for l in (1, 0, 2, 3)] for h in range(4) for c in range(2)]
    plane = [
        [(2 * z + c) * n_col + k for k in range(n_col) for c in range(2)] for z in range(n_row // 2)
    ]
    far = [[(4 * h + l) * 2 + c for h in range(4)] for l in range(4) for c in range(2)]
    swap = [(i, i ^ 1) for i in range(n_row)]
    scale = math.sqrt(rows * n_row * cols * n_col / rank)
    work = dict(flops=5 * 10**8, moved=2 * 10**6)

    blended, here, there = lax.optimization_barrier(
        (momentum + grad.astype(F32), core.reshape(1), 1 - core.reshape(1))
    )
    part = call(
        project_kernel, shape(1024, 128), blended, jnp.swapaxes(trailing_coefficients, 1, 2)
    )
    pieces = lax.all_to_all(part.reshape(n_col, 64, 128), "col", 0, 0)
    summed = call(sum_kernel, shape(n_col, 64, 128), pieces)
    projected = lax.all_to_all(summed, "col", 0, 0).reshape(1024, 128)

    def products(half):
        return call(
            products_kernel,
            shape(HALF_ROWS, 128),
            half,
            blended,
            projected,
            scalar=True,
            **work,
        )

    theirs = lax.ppermute(products(there), "row", swap)
    mine = products(here)
    pieces = call(pair_sum_kernel, shape(HALF_ROWS, 128), mine, theirs)
    quarter = HALF_ROWS // 4
    pieces = lax.all_to_all(
        pieces.reshape(4, quarter, 128), "row", 0, 0, axis_index_groups=near
    )
    summed = call(sum_kernel, shape(4, quarter, 128), pieces)
    pieces = lax.all_to_all(summed, "row", 0, 0, axis_index_groups=far)
    summed = call(sum_kernel, shape(4, quarter, 128), pieces)
    reduced = lax.all_to_all(summed, "row", 0, 0, axis_index_groups=near)

    mine, squares = call(
        factor_kernel,
        (shape(FACTOR_ROWS, 128), shape(2 * n_col, 8, 128)),
        reduced.reshape(HALF_ROWS, 128),
        scratch=(pltpu.VMEM(((FOUR + 1) * rank, 128), F32),) * 2,
    )
    theirs = lax.ppermute(mine, "row", swap)
    squares = lax.all_to_all(squares, ("row", "col"), 0, 0, axis_index_groups=plane)
    momentum_next, orthonormal = call(
        retain_kernel,
        (shape(mats, rows, cols), shape(mats, rows, 4 * rank, dtype=BF16)),
        here,
        mine,
        theirs,
        blended,
        projected,
        scalar=True,
        **work,
    )
    update, right = call(
        functools.partial(update_kernel, scale=scale),
        (shape(mats, rows, cols, dtype=BF16), shape(mats, rank, cols)),
        here,
        squares,
        mine,
        theirs,
        orthonormal,
        scalar=True,
    )
    return update, momentum_next, jnp.swapaxes(right, 1, 2)


def solution(mesh):
    return jax.shard_map(
        on_device,
        mesh=mesh,
        in_specs=(P(None, "row", "col"), P(None, "row", "col"), P(None, "col", None)),
        out_specs=(P(None, "row", "col"), P(None, "row", "col"), P(None, "col", None)),
        check_vma=False,
    )
```

```python
import functools
import math

import jax
import jax.numpy as jnp
from jax import lax
from jax.experimental import pallas as pl
from jax.experimental.pallas import tpu as pltpu
from jax.sharding import PartitionSpec as P

DECAY = 1.0 - 0.95
EPS = 1e-08
F32 = jnp.float32
BF16 = jnp.bfloat16
HUB = 10
NEAR = (2, 1, 3, 0)
FAR = (2, 0, 1, 3)
ORDER = ((0, 0), (0, 1), (1, 0), (1, 1), (0, 2), (2, 0))


def parts(x, count):
    out = []
    for _ in range(count):
        out.append(x.astype(BF16))
        x = x - out[-1].astype(F32)
    return out


def dot(a, b, ca=1, cb=0, terms=6):
    count = 3 if terms > 4 else 2
    a, b = parts(a, count), parts(b, count)
    return lax.dot_general(
        jnp.concatenate([a[i] for i, _ in ORDER[:terms]], axis=ca),
        jnp.concatenate([b[j] for _, j in ORDER[:terms]], axis=cb),
        (((ca,), (cb,)), ((), ())),
        preferred_element_type=F32,
    )


def project_kernel(b_ref, v_ref, p_ref):
    mats, rows, _ = b_ref.shape
    half = rows // 2
    for i in range(mats):
        p = dot(b_ref[i], v_ref[i], 1, 1, 3)
        p_ref[pl.ds(i * half, half), :] = jnp.concatenate([p[:half], p[half:]], axis=1)


def sum_kernel(x_ref, o_ref):
    total = x_ref[0]
    for i in range(1, x_ref.shape[0]):
        total = total + x_ref[i]
    for i in range(o_ref.shape[0]):
        o_ref[i] = total


def pair_sum_kernel(x_ref, y_ref, o_ref):
    o_ref[...] = x_ref[...] + y_ref[...]


RANK = 64
FOUR = 4
SHARED = FOUR * RANK
SQUARES = SHARED + RANK // 2
LAST = SQUARES + 2 * (RANK // 2)
HALF_ROWS = LAST + RANK // 2
INVERSES = SQUARES
FACTOR_ROWS = INVERSES + (FOUR + 1) * (RANK // 2)


def fold(x):
    return jnp.concatenate([x[: RANK // 2], x[RANK // 2 :]], axis=1)


def unfold(x):
    return jnp.concatenate([x[:, :RANK], x[:, RANK:]], axis=0)


def square_iota():
    row = lax.broadcasted_iota(jnp.int32, (RANK, RANK), 0)
    lane = lax.broadcasted_iota(jnp.int32, (RANK, RANK), 1)
    return row, lane


def products_kernel(h_ref, b_ref, p_ref, o_ref):
    mats, rows, _ = b_ref.shape
    half = rows // 2
    h = h_ref[0]
    row, lane = square_iota()
    grams = []
    for s in range(FOUR + 1):
        i = mats - 1 if s == FOUR else h * FOUR + s
        b = b_ref[i]
        at = i * half if s == FOUR else pl.multiple_of(i * half, 8)
        pp = p_ref[pl.ds(at, half), :]
        full = dot(pp, jnp.concatenate([b[:half], b[half:], pp], axis=1), 0, 0)
        y = full[:RANK, :128] + full[RANK:, 128:256]
        if s == FOUR:
            o_ref[pl.ds(SHARED, RANK // 2), :] = fold(jnp.where(h == 0, y[:, :RANK], y[:, RANK:]))
        else:
            o_ref[pl.ds(s * RANK, RANK), :] = y
        grams.append(full[:RANK, 256 : 256 + RANK] + full[RANK:, 256 + RANK :])
    quarter = RANK // 2
    row32 = lax.broadcasted_iota(jnp.int32, (quarter, quarter), 0)
    extra = jnp.zeros((quarter, quarter), F32)
    for t in range(2):
        lower, upper = grams[2 * t], grams[2 * t + 1]
        o_ref[pl.ds(SQUARES + t * quarter, quarter), :] = fold(jnp.where(lane <= row, lower, upper))
        diag = jnp.sum(jnp.where(lane == row, upper, 0.0), axis=0, keepdims=True)
        extra = jnp.where(row32 == 2 * t, diag[:, :quarter], extra)
        extra = jnp.where(row32 == 2 * t + 1, diag[:, quarter:], extra)
    last = grams[FOUR]
    o_ref[pl.ds(LAST, quarter), :] = jnp.concatenate(
        [last[:quarter, :quarter], last[quarter:], extra], axis=1
    )


def read_grams(gy_ref):
    quarter = RANK // 2
    row, lane = square_iota()
    last = gy_ref[pl.ds(LAST, quarter), :]
    extra = last[:, 3 * quarter :]
    grams = []
    for t in range(2):
        square = unfold(gy_ref[pl.ds(SQUARES + t * quarter, quarter), :])
        other = jnp.transpose(square)
        diag = jnp.concatenate([extra[2 * t : 2 * t + 1], extra[2 * t + 1 : 2 * t + 2]], axis=1)
        grams.append(jnp.where(lane <= row, square, other))
        grams.append(jnp.where(lane == row, diag, jnp.where(lane > row, square, other)))
    bottom = last[:, quarter : 3 * quarter]
    top = jnp.concatenate([last[:, :quarter], jnp.transpose(bottom[:, :quarter])], axis=1)
    grams.append(jnp.concatenate([top, bottom], axis=0))
    return grams


def factor_kernel(gy_ref, o_ref, n_ref, a_ref, h_ref):
    rank = RANK
    slots = FOUR + 1
    size = 16
    row, lane = square_iota()
    eye = jnp.where(lane == row, 1.0, 0.0).astype(F32)
    for s, gram in enumerate(read_grams(gy_ref)):
        a_ref[pl.ds(s * rank, rank), :] = jnp.concatenate([gram, eye], axis=1)
    for first in range(0, rank, size):
        a = [a_ref[pl.ds(first + p, slots, stride=rank), :] for p in range(size)]
        e = [
            [
                jnp.broadcast_to(a[i][:, first + j : first + j + 1], (slots, 128))
                for j in range(i + 1)
            ]
            for i in range(size)
        ]
        for p in range(size):
            root = lax.rsqrt(e[p][p])
            a[p] = a[p] * root
            low = [None] * size
            for i in range(p + 1, size):
                low[i] = e[i][p] * root
            for i in range(p + 1, size):
                for j in range(p + 1, i + 1):
                    e[i][j] = e[i][j] - low[i] * low[j]
                a[i] = a[i] - low[i] * a[p]
            h_ref[pl.ds(first + p, slots, stride=rank), :] = a[p]
        left = rank - first - size
        if left:
            for s in range(slots):
                h = h_ref[pl.ds(s * rank + first, size), :]
                at = pl.ds(s * rank + first + size, left)
                a_ref[at, :] = a_ref[at, :] - dot(h[:, first + size : rank], h, 0, 0)
    row8 = lax.broadcasted_iota(jnp.int32, (8, 128), 0)
    table = jnp.zeros((8, 128), F32)
    zero = jnp.zeros((8, rank), F32)
    for s in range(slots):
        inv = h_ref[pl.ds(s * rank, rank), :][:, rank:]
        if s == FOUR:
            xt = dot(inv, unfold(gy_ref[pl.ds(SHARED, rank // 2), :]))
            o_ref[pl.ds(SHARED, rank // 2), :] = fold(xt)
        else:
            xt = dot(inv, gy_ref[pl.ds(s * rank, rank), :])
            o_ref[pl.ds(s * rank, rank), :] = xt
        squares = dot(jnp.ones((8, xt.shape[1]), F32), xt * xt, 1, 1)
        table = jnp.where(row8 == s, jnp.concatenate([squares, zero], axis=1), table)
        o_ref[pl.ds(INVERSES + s * (rank // 2), rank // 2), :] = fold(inv)
    for c in range(n_ref.shape[0]):
        n_ref[c] = table


def read_crossed(core, i, mine_ref, theirs_ref):
    h, s = divmod(i, FOUR)
    if h < 2:
        at = pl.ds(s * RANK, RANK)
        return jnp.where(core == h, mine_ref[at, :], theirs_ref[at, :])
    at = pl.ds(SHARED, RANK // 2)
    mine, theirs = unfold(mine_ref[at, :]), unfold(theirs_ref[at, :])
    return jnp.concatenate(
        [jnp.where(core == 0, mine, theirs), jnp.where(core == 0, theirs, mine)], axis=1
    )


def retain_kernel(core_ref, mine_ref, theirs_ref, b_ref, p_ref, mo_ref, q_ref):
    mats, rows, _ = b_ref.shape
    half = rows // 2
    core = core_ref[0]
    for i in range(mats):
        h, s = divmod(i, FOUR)
        xt = read_crossed(core, i, mine_ref, theirs_ref)
        if h < 2:
            at = pl.ds(INVERSES + s * (RANK // 2), RANK // 2)
            inv = unfold(jnp.where(core == h, mine_ref[at, :], theirs_ref[at, :]))
        else:
            inv = unfold(mine_ref[pl.ds(INVERSES + FOUR * (RANK // 2), RANK // 2), :])
        p = unfold(p_ref[pl.ds(i * half, half), :])
        qh, ql = parts(dot(p, inv, 1, 1, 4), 2)
        q = jnp.concatenate([qh, qh, ql, ql], axis=1)
        q_ref[i] = q
        xh, xl = parts(xt, 2)
        low_rank = jnp.dot(
            q, jnp.concatenate([xh, xl, xh, xl], axis=0), preferred_element_type=F32
        )
        mo_ref[i] = b_ref[i] - DECAY * low_rank


def update_kernel(core_ref, n_ref, mine_ref, theirs_ref, q_ref, u_ref, r_ref, *, scale):
    mats = q_ref.shape[0]
    core = core_ref[0]
    totals = [n_ref[0], n_ref[1]]
    for i in range(2, n_ref.shape[0]):
        totals[i % 2] = totals[i % 2] + n_ref[i]
    row = lax.broadcasted_iota(jnp.int32, totals[0].shape, 0)
    totals[0] = jnp.where(row == FOUR, totals[0] + totals[1], totals[0])
    total = jnp.concatenate(totals, axis=0)
    inverse = 1.0 / (jnp.sqrt(jnp.transpose(total)) + EPS)
    for i in range(mats):
        h, s = divmod(i, FOUR)
        xt = read_crossed(core, i, mine_ref, theirs_ref)
        at = 8 * h + s if h < 2 else FOUR
        rt = xt * inverse[:RANK, at : at + 1]
        r_ref[i] = rt
        rh, rl = parts(scale * rt, 2)
        u_ref[i] = jnp.dot(
            q_ref[i], jnp.concatenate([rh, rl, rh, rl], axis=0), preferred_element_type=F32
        ).astype(BF16)


def call(kernel, out, *args, scalar=False, scratch=(), flops=0, moved=0):
    vmem = pl.BlockSpec(memory_space=pltpu.VMEM)
    first = pl.BlockSpec(memory_space=pltpu.SMEM) if scalar else vmem
    return pl.pallas_call(
        kernel,
        out_shape=out,
        in_specs=(first,) + (vmem,) * (len(args) - 1),
        out_specs=(vmem,) * len(out) if isinstance(out, tuple) else vmem,
        scratch_shapes=scratch,
        cost_estimate=pl.CostEstimate(flops=flops, bytes_accessed=moved, transcendentals=0),
        compiler_params=pltpu.CompilerParams(vmem_limit_bytes=32 * 1024 * 1024),
    )(*args)


def shape(*dims, dtype=F32):
    return jax.ShapeDtypeStruct(dims, dtype)


def on_device(grad, momentum, trailing_coefficients):
    mats, rows, cols = momentum.shape
    rank = trailing_coefficients.shape[2]
    n_col = lax.axis_size("col")
    n_row = lax.axis_size("row")
    core = lax.rem(lax.axis_index("row"), 2)
    near = [[(4 * h + l) * 2 + c for l in NEAR] for h in range(4) for c in range(2)]
    order = [HUB, *(k for k in range(n_col) if k != HUB)]
    plane = [[(2 * z + c) * n_col + k for k in order for c in range(2)] for z in range(n_row // 2)]
    far = [[(4 * h + l) * 2 + c for h in FAR] for l in range(4) for c in range(2)]
    swap = [(i, i ^ 1) for i in range(n_row)]
    scale = math.sqrt(rows * n_row * cols * n_col / rank)
    work = dict(flops=5 * 10**8, moved=2 * 10**6)

    blended, here, there = lax.optimization_barrier(
        (momentum + grad.astype(F32), core.reshape(1), 1 - core.reshape(1))
    )
    part = call(
        project_kernel, shape(1024, 128), blended, jnp.swapaxes(trailing_coefficients, 1, 2)
    )
    pieces = lax.all_to_all(
        part.reshape(n_col, 64, 128), "col", 0, 0, axis_index_groups=[order]
    )
    summed = call(sum_kernel, shape(n_col, 64, 128), pieces)
    projected = lax.all_to_all(summed, "col", 0, 0, axis_index_groups=[order])
    projected = projected.reshape(1024, 128)

    def products(half):
        return call(
            products_kernel,
            shape(HALF_ROWS, 128),
            half,
            blended,
            projected,
            scalar=True,
            **work,
        )

    theirs = lax.ppermute(products(there), "row", swap)
    mine = products(here)
    pieces = call(pair_sum_kernel, shape(HALF_ROWS, 128), mine, theirs)
    quarter = HALF_ROWS // 4
    pieces = lax.all_to_all(
        pieces.reshape(4, quarter, 128), "row", 0, 0, axis_index_groups=near
    )
    summed = call(sum_kernel, shape(4, quarter, 128), pieces)
    pieces = lax.all_to_all(summed, "row", 0, 0, axis_index_groups=far)
    summed = call(sum_kernel, shape(4, quarter, 128), pieces)
    reduced = lax.all_to_all(summed, "row", 0, 0, axis_index_groups=near)

    mine, squares = call(
        factor_kernel,
        (shape(FACTOR_ROWS, 128), shape(2 * n_col, 8, 128)),
        reduced.reshape(HALF_ROWS, 128),
        scratch=(pltpu.VMEM(((FOUR + 1) * rank, 128), F32),) * 2,
    )
    theirs = lax.ppermute(mine, "row", swap)
    squares = lax.all_to_all(squares, ("row", "col"), 0, 0, axis_index_groups=plane)
    momentum_next, orthonormal = call(
        retain_kernel,
        (shape(mats, rows, cols), shape(mats, rows, 4 * rank, dtype=BF16)),
        here,
        mine,
        theirs,
        blended,
        projected,
        scalar=True,
        **work,
    )
    update, right = call(
        functools.partial(update_kernel, scale=scale),
        (shape(mats, rows, cols, dtype=BF16), shape(mats, rank, cols)),
        here,
        squares,
        mine,
        theirs,
        orthonormal,
        scalar=True,
    )
    return update, momentum_next, jnp.swapaxes(right, 1, 2)


def solution(mesh):
    return jax.shard_map(
        on_device,
        mesh=mesh,
        in_specs=(P(None, "row", "col"), P(None, "row", "col"), P(None, "col", None)),
        out_specs=(P(None, "row", "col"), P(None, "row", "col"), P(None, "col", None)),
        check_vma=False,
    )
```

```python
import functools
import math

import jax
import jax.numpy as jnp
from jax import lax
from jax.experimental import pallas as pl
from jax.experimental.pallas import tpu as pltpu
from jax.sharding import PartitionSpec as P

DECAY = 1.0 - 0.95
EPS = 1e-08
F32 = jnp.float32
BF16 = jnp.bfloat16
HUB = 10
NEAR = (2, 1, 3, 0)
FAR = (2, 0, 1, 3)
ORDER = ((0, 0), (0, 1), (1, 0), (1, 1), (0, 2), (2, 0))


def parts(x, count):
    out = []
    for _ in range(count):
        out.append(x.astype(BF16))
        x = x - out[-1].astype(F32)
    return out


def dot(a, b, ca=1, cb=0, terms=6):
    count = 3 if terms > 4 else 2
    a, b = parts(a, count), parts(b, count)
    return lax.dot_general(
        jnp.concatenate([a[i] for i, _ in ORDER[:terms]], axis=ca),
        jnp.concatenate([b[j] for _, j in ORDER[:terms]], axis=cb),
        (((ca,), (cb,)), ((), ())),
        preferred_element_type=F32,
    )


def project_kernel(b_ref, v_ref, p_ref):
    mats, rows, _ = b_ref.shape
    half = rows // 2
    for i in range(mats):
        p = dot(b_ref[i], v_ref[i], 1, 1, 3)
        p_ref[pl.ds(i * half, half), :] = jnp.concatenate([p[:half], p[half:]], axis=1)
    rest = p_ref.shape[0] - mats * half
    p_ref[pl.ds(mats * half, rest), :] = jnp.zeros((rest, 128), F32)


def sum_kernel(x_ref, o_ref):
    total = x_ref[0]
    for i in range(1, x_ref.shape[0]):
        total = total + x_ref[i]
    for i in range(o_ref.shape[0]):
        o_ref[i] = total


def pair_sum_kernel(x_ref, y_ref, o_ref):
    o_ref[...] = x_ref[...] + y_ref[...]


RANK = 64
FOUR = 4
SHARED = FOUR * RANK
SQUARES = SHARED + RANK // 2
LAST = SQUARES + 2 * (RANK // 2)
HALF_ROWS = LAST + RANK // 2
INVERSES = SQUARES
FACTOR_ROWS = INVERSES + (FOUR + 1) * (RANK // 2)


def fold(x):
    return jnp.concatenate([x[: RANK // 2], x[RANK // 2 :]], axis=1)


def unfold(x):
    return jnp.concatenate([x[:, :RANK], x[:, RANK:]], axis=0)


def square_iota():
    row = lax.broadcasted_iota(jnp.int32, (RANK, RANK), 0)
    lane = lax.broadcasted_iota(jnp.int32, (RANK, RANK), 1)
    return row, lane


def products_kernel(h_ref, b_ref, p_ref, o_ref):
    mats, rows, _ = b_ref.shape
    half = rows // 2
    h = h_ref[0]
    row, lane = square_iota()
    grams = []
    for s in range(FOUR + 1):
        i = mats - 1 if s == FOUR else h * FOUR + s
        b = b_ref[i]
        at = i * half if s == FOUR else pl.multiple_of(i * half, 8)
        pp = p_ref[pl.ds(at, half), :]
        full = dot(pp, jnp.concatenate([b[:half], b[half:], pp], axis=1), 0, 0)
        y = full[:RANK, :128] + full[RANK:, 128:256]
        if s == FOUR:
            o_ref[pl.ds(SHARED, RANK // 2), :] = fold(jnp.where(h == 0, y[:, :RANK], y[:, RANK:]))
        else:
            o_ref[pl.ds(s * RANK, RANK), :] = y
        grams.append(full[:RANK, 256 : 256 + RANK] + full[RANK:, 256 + RANK :])
    quarter = RANK // 2
    row32 = lax.broadcasted_iota(jnp.int32, (quarter, quarter), 0)
    extra = jnp.zeros((quarter, quarter), F32)
    for t in range(2):
        lower, upper = grams[2 * t], grams[2 * t + 1]
        o_ref[pl.ds(SQUARES + t * quarter, quarter), :] = fold(jnp.where(lane <= row, lower, upper))
        diag = jnp.sum(jnp.where(lane == row, upper, 0.0), axis=0, keepdims=True)
        extra = jnp.where(row32 == 2 * t, diag[:, :quarter], extra)
        extra = jnp.where(row32 == 2 * t + 1, diag[:, quarter:], extra)
    last = grams[FOUR]
    o_ref[pl.ds(LAST, quarter), :] = jnp.concatenate(
        [last[:quarter, :quarter], last[quarter:], extra], axis=1
    )


def read_grams(gy_ref):
    quarter = RANK // 2
    row, lane = square_iota()
    last = gy_ref[pl.ds(LAST, quarter), :]
    extra = last[:, 3 * quarter :]
    grams = []
    for t in range(2):
        square = unfold(gy_ref[pl.ds(SQUARES + t * quarter, quarter), :])
        other = jnp.transpose(square)
        diag = jnp.concatenate([extra[2 * t : 2 * t + 1], extra[2 * t + 1 : 2 * t + 2]], axis=1)
        grams.append(jnp.where(lane <= row, square, other))
        grams.append(jnp.where(lane == row, diag, jnp.where(lane > row, square, other)))
    bottom = last[:, quarter : 3 * quarter]
    top = jnp.concatenate([last[:, :quarter], jnp.transpose(bottom[:, :quarter])], axis=1)
    grams.append(jnp.concatenate([top, bottom], axis=0))
    return grams


def factor_kernel(gy_ref, o_ref, n_ref, a_ref, h_ref):
    rank = RANK
    slots = FOUR + 1
    size = 16
    row, lane = square_iota()
    eye = jnp.where(lane == row, 1.0, 0.0).astype(F32)
    for s, gram in enumerate(read_grams(gy_ref)):
        a_ref[pl.ds(s * rank, rank), :] = jnp.concatenate([gram, eye], axis=1)
    for first in range(0, rank, size):
        a = [a_ref[pl.ds(first + p, slots, stride=rank), :] for p in range(size)]
        e = [
            [
                jnp.broadcast_to(a[i][:, first + j : first + j + 1], (slots, 128))
                for j in range(i + 1)
            ]
            for i in range(size)
        ]
        for p in range(size):
            root = lax.rsqrt(e[p][p])
            a[p] = a[p] * root
            low = [None] * size
            for i in range(p + 1, size):
                low[i] = e[i][p] * root
            for i in range(p + 1, size):
                for j in range(p + 1, i + 1):
                    e[i][j] = e[i][j] - low[i] * low[j]
                a[i] = a[i] - low[i] * a[p]
            h_ref[pl.ds(first + p, slots, stride=rank), :] = a[p]
        left = rank - first - size
        if left:
            for s in range(slots):
                h = h_ref[pl.ds(s * rank + first, size), :]
                at = pl.ds(s * rank + first + size, left)
                a_ref[at, :] = a_ref[at, :] - dot(h[:, first + size : rank], h, 0, 0)
    row8 = lax.broadcasted_iota(jnp.int32, (8, 128), 0)
    table = jnp.zeros((8, 128), F32)
    zero = jnp.zeros((8, rank), F32)
    for s in range(slots):
        inv = h_ref[pl.ds(s * rank, rank), :][:, rank:]
        if s == FOUR:
            xt = dot(inv, unfold(gy_ref[pl.ds(SHARED, rank // 2), :]))
            o_ref[pl.ds(SHARED, rank // 2), :] = fold(xt)
        else:
            xt = dot(inv, gy_ref[pl.ds(s * rank, rank), :])
            o_ref[pl.ds(s * rank, rank), :] = xt
        squares = dot(jnp.ones((8, xt.shape[1]), F32), xt * xt, 1, 1)
        table = jnp.where(row8 == s, jnp.concatenate([squares, zero], axis=1), table)
        o_ref[pl.ds(INVERSES + s * (rank // 2), rank // 2), :] = fold(inv)
    for c in range(n_ref.shape[0]):
        n_ref[c] = table


def read_crossed(core, i, mine_ref, theirs_ref):
    h, s = divmod(i, FOUR)
    if h < 2:
        at = pl.ds(s * RANK, RANK)
        return jnp.where(core == h, mine_ref[at, :], theirs_ref[at, :])
    at = pl.ds(SHARED, RANK // 2)
    mine, theirs = unfold(mine_ref[at, :]), unfold(theirs_ref[at, :])
    return jnp.concatenate(
        [jnp.where(core == 0, mine, theirs), jnp.where(core == 0, theirs, mine)], axis=1
    )


def retain_kernel(core_ref, mine_ref, theirs_ref, b_ref, p_ref, mo_ref, q_ref):
    mats, rows, _ = b_ref.shape
    half = rows // 2
    core = core_ref[0]
    for i in range(mats):
        h, s = divmod(i, FOUR)
        xt = read_crossed(core, i, mine_ref, theirs_ref)
        if h < 2:
            at = pl.ds(INVERSES + s * (RANK // 2), RANK // 2)
            inv = unfold(jnp.where(core == h, mine_ref[at, :], theirs_ref[at, :]))
        else:
            inv = unfold(mine_ref[pl.ds(INVERSES + FOUR * (RANK // 2), RANK // 2), :])
        p = unfold(p_ref[pl.ds(i * half, half), :])
        qh, ql = parts(dot(p, inv, 1, 1, 4), 2)
        q = jnp.concatenate([qh, qh, ql, ql], axis=1)
        q_ref[i] = q
        xh, xl = parts(xt, 2)
        low_rank = jnp.dot(
            q, jnp.concatenate([xh, xl, xh, xl], axis=0), preferred_element_type=F32
        )
        mo_ref[i] = b_ref[i] - DECAY * low_rank


def update_kernel(core_ref, n_ref, mine_ref, theirs_ref, q_ref, u_ref, r_ref, *, scale):
    mats = q_ref.shape[0]
    core = core_ref[0]
    totals = [n_ref[0], n_ref[1]]
    for i in range(2, n_ref.shape[0]):
        totals[i % 2] = totals[i % 2] + n_ref[i]
    row = lax.broadcasted_iota(jnp.int32, totals[0].shape, 0)
    totals[0] = jnp.where(row == FOUR, totals[0] + totals[1], totals[0])
    total = jnp.concatenate(totals, axis=0)
    inverse = 1.0 / (jnp.sqrt(jnp.transpose(total)) + EPS)
    for i in range(mats):
        h, s = divmod(i, FOUR)
        xt = read_crossed(core, i, mine_ref, theirs_ref)
        at = 8 * h + s if h < 2 else FOUR
        rt = xt * inverse[:RANK, at : at + 1]
        r_ref[i] = rt
        rh, rl = parts(scale * rt, 2)
        u_ref[i] = jnp.dot(
            q_ref[i], jnp.concatenate([rh, rl, rh, rl], axis=0), preferred_element_type=F32
        ).astype(BF16)


def call(kernel, out, *args, scalar=False, scratch=(), flops=0, moved=0):
    vmem = pl.BlockSpec(memory_space=pltpu.VMEM)
    first = pl.BlockSpec(memory_space=pltpu.SMEM) if scalar else vmem
    return pl.pallas_call(
        kernel,
        out_shape=out,
        in_specs=(first,) + (vmem,) * (len(args) - 1),
        out_specs=(vmem,) * len(out) if isinstance(out, tuple) else vmem,
        scratch_shapes=scratch,
        cost_estimate=pl.CostEstimate(flops=flops, bytes_accessed=moved, transcendentals=0),
        compiler_params=pltpu.CompilerParams(vmem_limit_bytes=32 * 1024 * 1024),
    )(*args)


def shape(*dims, dtype=F32):
    return jax.ShapeDtypeStruct(dims, dtype)


def on_device(grad, momentum, trailing_coefficients):
    mats, rows, cols = momentum.shape
    rank = trailing_coefficients.shape[2]
    n_col = lax.axis_size("col")
    n_row = lax.axis_size("row")
    core = lax.rem(lax.axis_index("row"), 2)
    near = [[(4 * h + l) * 2 + c for l in NEAR] for h in range(4) for c in range(2)]
    order = [HUB, *(k for k in range(n_col) if k != HUB)]
    plane = [[(2 * z + c) * n_col + k for k in order for c in range(2)] for z in range(n_row // 2)]
    far = [[(4 * h + l) * 2 + c for h in FAR] for l in range(4) for c in range(2)]
    swap = [(i, i ^ 1) for i in range(n_row)]
    scale = math.sqrt(rows * n_row * cols * n_col / rank)
    work = dict(flops=5 * 10**8, moved=2 * 10**6)

    blended, here, there = lax.optimization_barrier(
        (momentum + grad.astype(F32), core.reshape(1), 1 - core.reshape(1))
    )
    part = call(
        project_kernel, shape(1024, 128), blended, jnp.swapaxes(trailing_coefficients, 1, 2)
    )
    pieces = lax.all_to_all(
        part.reshape(n_col, 64, 128), "col", 0, 0, axis_index_groups=[order]
    )
    summed = call(sum_kernel, shape(n_col, 64, 128), pieces)
    projected = lax.all_to_all(summed, "col", 0, 0, axis_index_groups=[order])
    projected = projected.reshape(1024, 128)

    def products(half):
        return call(
            products_kernel,
            shape(HALF_ROWS, 128),
            half,
            blended,
            projected,
            scalar=True,
            **work,
        )

    theirs = lax.ppermute(products(there), "row", swap)
    mine = products(here)
    pieces = call(pair_sum_kernel, shape(HALF_ROWS, 128), mine, theirs)
    quarter = HALF_ROWS // 4
    pieces = lax.all_to_all(
        pieces.reshape(4, quarter, 128), "row", 0, 0, axis_index_groups=near
    )
    summed = call(sum_kernel, shape(4, quarter, 128), pieces)
    pieces = lax.all_to_all(summed, "row", 0, 0, axis_index_groups=far)
    summed = call(sum_kernel, shape(4, quarter, 128), pieces)
    reduced = lax.all_to_all(summed, "row", 0, 0, axis_index_groups=near)

    mine, squares = call(
        factor_kernel,
        (shape(FACTOR_ROWS, 128), shape(2 * n_col, 8, 128)),
        reduced.reshape(HALF_ROWS, 128),
        scratch=(pltpu.VMEM((8 * rank, 128), F32),) * 2,
    )
    theirs = lax.ppermute(mine, "row", swap)
    squares = lax.all_to_all(squares, ("row", "col"), 0, 0, axis_index_groups=plane)
    momentum_next, orthonormal = call(
        retain_kernel,
        (shape(mats, rows, cols), shape(mats, rows, 4 * rank, dtype=BF16)),
        here,
        mine,
        theirs,
        blended,
        projected,
        scalar=True,
        **work,
    )
    update, right = call(
        functools.partial(update_kernel, scale=scale),
        (shape(mats, rows, cols, dtype=BF16), shape(mats, rank, cols)),
        here,
        squares,
        mine,
        theirs,
        orthonormal,
        scalar=True,
    )
    return update, momentum_next, jnp.swapaxes(right, 1, 2)


def solution(mesh):
    return jax.shard_map(
        on_device,
        mesh=mesh,
        in_specs=(P(None, "row", "col"), P(None, "row", "col"), P(None, "col", None)),
        out_specs=(P(None, "row", "col"), P(None, "row", "col"), P(None, "col", None)),
        check_vma=False,
    )
```

```python
import functools
import math

import jax
import jax.numpy as jnp
from jax import lax
from jax.experimental import pallas as pl
from jax.experimental.pallas import tpu as pltpu
from jax.sharding import PartitionSpec as P

DECAY = 1.0 - 0.95
EPS = 1e-08
F32 = jnp.float32
BF16 = jnp.bfloat16
HUB = 10
NEAR = (2, 1, 3, 0)
FAR = (2, 0, 1, 3)
ORDER = ((0, 0), (0, 1), (1, 0), (1, 1), (0, 2), (2, 0))


def parts(x, count):
    out = []
    for _ in range(count):
        out.append(x.astype(BF16))
        x = x - out[-1].astype(F32)
    return out


def dot(a, b, ca=1, cb=0, terms=6):
    count = 3 if terms > 4 else 2
    a, b = parts(a, count), parts(b, count)
    return lax.dot_general(
        jnp.concatenate([a[i] for i, _ in ORDER[:terms]], axis=ca),
        jnp.concatenate([b[j] for _, j in ORDER[:terms]], axis=cb),
        (((ca,), (cb,)), ((), ())),
        preferred_element_type=F32,
    )


def project_kernel(b_ref, v_ref, p_ref):
    mats, rows, _ = b_ref.shape
    half = rows // 2
    for i in range(mats):
        p = dot(b_ref[i], v_ref[i], 1, 1, 3)
        p_ref[pl.ds(i * half, half), :] = jnp.concatenate([p[:half], p[half:]], axis=1)
    rest = p_ref.shape[0] - mats * half
    p_ref[pl.ds(mats * half, rest), :] = jnp.zeros((rest, 128), F32)


def sum_kernel(x_ref, o_ref):
    total = x_ref[0]
    for i in range(1, x_ref.shape[0]):
        total = total + x_ref[i]
    for i in range(o_ref.shape[0]):
        o_ref[i] = total


def pair_sum_kernel(x_ref, y_ref, o_ref):
    o_ref[...] = x_ref[...] + y_ref[...]


RANK = 64
FOUR = 4
SHARED = FOUR * RANK
SQUARES = SHARED + RANK // 2
LAST = SQUARES + 2 * (RANK // 2)
HALF_ROWS = LAST + RANK // 2
INVERSES = SQUARES
FACTOR_ROWS = INVERSES + (FOUR + 1) * (RANK // 2)


def fold(x):
    return jnp.concatenate([x[: RANK // 2], x[RANK // 2 :]], axis=1)


def unfold(x):
    return jnp.concatenate([x[:, :RANK], x[:, RANK:]], axis=0)


def square_iota():
    row = lax.broadcasted_iota(jnp.int32, (RANK, RANK), 0)
    lane = lax.broadcasted_iota(jnp.int32, (RANK, RANK), 1)
    return row, lane


def products_kernel(h_ref, b_ref, p_ref, o_ref):
    mats, rows, _ = b_ref.shape
    half = rows // 2
    h = h_ref[0]
    row, lane = square_iota()
    grams = []
    for s in range(FOUR + 1):
        i = mats - 1 if s == FOUR else h * FOUR + s
        b = b_ref[i]
        at = i * half if s == FOUR else pl.multiple_of(i * half, 8)
        pp = p_ref[pl.ds(at, half), :]
        full = dot(pp, jnp.concatenate([b[:half], b[half:], pp], axis=1), 0, 0)
        y = full[:RANK, :128] + full[RANK:, 128:256]
        if s == FOUR:
            o_ref[pl.ds(SHARED, RANK // 2), :] = fold(jnp.where(h == 0, y[:, :RANK], y[:, RANK:]))
        else:
            o_ref[pl.ds(s * RANK, RANK), :] = y
        grams.append(full[:RANK, 256 : 256 + RANK] + full[RANK:, 256 + RANK :])
    quarter = RANK // 2
    row32 = lax.broadcasted_iota(jnp.int32, (quarter, quarter), 0)
    extra = jnp.zeros((quarter, quarter), F32)
    for t in range(2):
        lower, upper = grams[2 * t], grams[2 * t + 1]
        o_ref[pl.ds(SQUARES + t * quarter, quarter), :] = fold(jnp.where(lane <= row, lower, upper))
        diag = jnp.sum(jnp.where(lane == row, upper, 0.0), axis=0, keepdims=True)
        extra = jnp.where(row32 == 2 * t, diag[:, :quarter], extra)
        extra = jnp.where(row32 == 2 * t + 1, diag[:, quarter:], extra)
    last = grams[FOUR]
    o_ref[pl.ds(LAST, quarter), :] = jnp.concatenate(
        [last[:quarter, :quarter], last[quarter:], extra], axis=1
    )


def read_grams(gy_ref):
    quarter = RANK // 2
    row, lane = square_iota()
    last = gy_ref[pl.ds(LAST, quarter), :]
    extra = last[:, 3 * quarter :]
    grams = []
    for t in range(2):
        square = unfold(gy_ref[pl.ds(SQUARES + t * quarter, quarter), :])
        other = jnp.transpose(square)
        diag = jnp.concatenate([extra[2 * t : 2 * t + 1], extra[2 * t + 1 : 2 * t + 2]], axis=1)
        grams.append(jnp.where(lane <= row, square, other))
        grams.append(jnp.where(lane == row, diag, jnp.where(lane > row, square, other)))
    bottom = last[:, quarter : 3 * quarter]
    top = jnp.concatenate([last[:, :quarter], jnp.transpose(bottom[:, :quarter])], axis=1)
    grams.append(jnp.concatenate([top, bottom], axis=0))
    return grams


def factor_kernel(gy_ref, o_ref, n_ref, a_ref, h_ref):
    rank = RANK
    slots = FOUR + 1
    size = 16
    row, lane = square_iota()
    eye = jnp.where(lane == row, 1.0, 0.0).astype(F32)
    for s, gram in enumerate(read_grams(gy_ref)):
        a_ref[pl.ds(s * rank, rank), :] = jnp.concatenate([gram, eye], axis=1)
    for first in range(0, rank, size):
        a = [a_ref[pl.ds(first + p, slots, stride=rank), :] for p in range(size)]
        e = [
            [
                jnp.broadcast_to(a[i][:, first + j : first + j + 1], (slots, 128))
                for j in range(i + 1)
            ]
            for i in range(size)
        ]
        for p in range(size):
            root = lax.rsqrt(e[p][p])
            a[p] = a[p] * root
            low = [None] * size
            for i in range(p + 1, size):
                low[i] = e[i][p] * root
            for i in range(p + 1, size):
                for j in range(p + 1, i + 1):
                    e[i][j] = e[i][j] - low[i] * low[j]
                a[i] = a[i] - low[i] * a[p]
            h_ref[pl.ds(first + p, slots, stride=rank), :] = a[p]
        left = rank - first - size
        if left:
            for s in range(slots):
                h = h_ref[pl.ds(s * rank + first, size), :]
                at = pl.ds(s * rank + first + size, left)
                a_ref[at, :] = a_ref[at, :] - dot(h[:, first + size : rank], h, 0, 0)
    row8 = lax.broadcasted_iota(jnp.int32, (8, 128), 0)
    table = jnp.zeros((8, 128), F32)
    zero = jnp.zeros((8, rank), F32)
    for s in range(slots):
        inv = h_ref[pl.ds(s * rank, rank), :][:, rank:]
        if s == FOUR:
            xt = dot(inv, unfold(gy_ref[pl.ds(SHARED, rank // 2), :]))
            o_ref[pl.ds(SHARED, rank // 2), :] = fold(xt)
        else:
            xt = dot(inv, gy_ref[pl.ds(s * rank, rank), :])
            o_ref[pl.ds(s * rank, rank), :] = xt
        pieces = jnp.concatenate(parts(xt * xt, 3), axis=1)
        squares = lax.dot_general(
            jnp.ones((8, pieces.shape[1]), BF16),
            pieces,
            (((1,), (1,)), ((), ())),
            preferred_element_type=F32,
        )
        table = jnp.where(row8 == s, jnp.concatenate([squares, zero], axis=1), table)
        o_ref[pl.ds(INVERSES + s * (rank // 2), rank // 2), :] = fold(inv)
    for c in range(n_ref.shape[0]):
        n_ref[c] = table


def read_crossed(core, i, mine_ref, theirs_ref):
    h, s = divmod(i, FOUR)
    if h < 2:
        at = pl.ds(s * RANK, RANK)
        return jnp.where(core == h, mine_ref[at, :], theirs_ref[at, :])
    at = pl.ds(SHARED, RANK // 2)
    mine, theirs = unfold(mine_ref[at, :]), unfold(theirs_ref[at, :])
    return jnp.concatenate(
        [jnp.where(core == 0, mine, theirs), jnp.where(core == 0, theirs, mine)], axis=1
    )


def retain_kernel(core_ref, mine_ref, theirs_ref, b_ref, p_ref, mo_ref, q_ref):
    mats, rows, _ = b_ref.shape
    half = rows // 2
    core = core_ref[0]
    for i in range(mats):
        h, s = divmod(i, FOUR)
        xt = read_crossed(core, i, mine_ref, theirs_ref)
        if h < 2:
            at = pl.ds(INVERSES + s * (RANK // 2), RANK // 2)
            inv = unfold(jnp.where(core == h, mine_ref[at, :], theirs_ref[at, :]))
        else:
            inv = unfold(mine_ref[pl.ds(INVERSES + FOUR * (RANK // 2), RANK // 2), :])
        p = unfold(p_ref[pl.ds(i * half, half), :])
        qh, ql = parts(dot(p, inv, 1, 1, 4), 2)
        q = jnp.concatenate([qh, qh, ql, ql], axis=1)
        q_ref[i] = q
        xh, xl = parts(xt, 2)
        low_rank = jnp.dot(
            q, jnp.concatenate([xh, xl, xh, xl], axis=0), preferred_element_type=F32
        )
        mo_ref[i] = b_ref[i] - DECAY * low_rank


def update_kernel(core_ref, n_ref, mine_ref, theirs_ref, q_ref, u_ref, r_ref, *, scale):
    mats = q_ref.shape[0]
    core = core_ref[0]
    totals = [n_ref[0], n_ref[1]]
    for i in range(2, n_ref.shape[0]):
        totals[i % 2] = totals[i % 2] + n_ref[i]
    row = lax.broadcasted_iota(jnp.int32, totals[0].shape, 0)
    totals[0] = jnp.where(row == FOUR, totals[0] + totals[1], totals[0])
    total = jnp.concatenate(totals, axis=0)
    inverse = 1.0 / (jnp.sqrt(jnp.transpose(total)) + EPS)
    for i in range(mats):
        h, s = divmod(i, FOUR)
        xt = read_crossed(core, i, mine_ref, theirs_ref)
        at = 8 * h + s if h < 2 else FOUR
        rt = xt * inverse[:RANK, at : at + 1]
        r_ref[i] = rt
        rh, rl = parts(scale * rt, 2)
        u_ref[i] = jnp.dot(
            q_ref[i], jnp.concatenate([rh, rl, rh, rl], axis=0), preferred_element_type=F32
        ).astype(BF16)


def call(kernel, out, *args, scalar=False, scratch=(), flops=0, moved=0):
    vmem = pl.BlockSpec(memory_space=pltpu.VMEM)
    first = pl.BlockSpec(memory_space=pltpu.SMEM) if scalar else vmem
    return pl.pallas_call(
        kernel,
        out_shape=out,
        in_specs=(first,) + (vmem,) * (len(args) - 1),
        out_specs=(vmem,) * len(out) if isinstance(out, tuple) else vmem,
        scratch_shapes=scratch,
        cost_estimate=pl.CostEstimate(flops=flops, bytes_accessed=moved, transcendentals=0),
        compiler_params=pltpu.CompilerParams(vmem_limit_bytes=32 * 1024 * 1024),
    )(*args)


def shape(*dims, dtype=F32):
    return jax.ShapeDtypeStruct(dims, dtype)


def on_device(grad, momentum, trailing_coefficients):
    mats, rows, cols = momentum.shape
    rank = trailing_coefficients.shape[2]
    n_col = lax.axis_size("col")
    n_row = lax.axis_size("row")
    core = lax.rem(lax.axis_index("row"), 2)
    near = [[(4 * h + l) * 2 + c for l in NEAR] for h in range(4) for c in range(2)]
    order = [HUB, *(k for k in range(n_col) if k != HUB)]
    plane = [[(2 * z + c) * n_col + k for k in order for c in range(2)] for z in range(n_row // 2)]
    far = [[(4 * h + l) * 2 + c for h in FAR] for l in range(4) for c in range(2)]
    swap = [(i, i ^ 1) for i in range(n_row)]
    scale = math.sqrt(rows * n_row * cols * n_col / rank)
    work = dict(flops=5 * 10**8, moved=2 * 10**6)

    blended, here, there = lax.optimization_barrier(
        (momentum + grad.astype(F32), core.reshape(1), 1 - core.reshape(1))
    )
    part = call(
        project_kernel, shape(1024, 128), blended, jnp.swapaxes(trailing_coefficients, 1, 2)
    )
    pieces = lax.all_to_all(
        part.reshape(n_col, 64, 128), "col", 0, 0, axis_index_groups=[order]
    )
    summed = call(sum_kernel, shape(n_col, 64, 128), pieces)
    projected = lax.all_to_all(summed, "col", 0, 0, axis_index_groups=[order])
    projected = projected.reshape(1024, 128)

    def products(half):
        return call(
            products_kernel,
            shape(HALF_ROWS, 128),
            half,
            blended,
            projected,
            scalar=True,
            **work,
        )

    theirs = lax.ppermute(products(there), "row", swap)
    mine = products(here)
    pieces = call(pair_sum_kernel, shape(HALF_ROWS, 128), mine, theirs)
    quarter = HALF_ROWS // 4
    pieces = lax.all_to_all(
        pieces.reshape(4, quarter, 128), "row", 0, 0, axis_index_groups=near
    )
    summed = call(sum_kernel, shape(4, quarter, 128), pieces)
    pieces = lax.all_to_all(summed, "row", 0, 0, axis_index_groups=far)
    summed = call(sum_kernel, shape(4, quarter, 128), pieces)
    reduced = lax.all_to_all(summed, "row", 0, 0, axis_index_groups=near)

    mine, squares = call(
        factor_kernel,
        (shape(FACTOR_ROWS, 128), shape(2 * n_col, 8, 128)),
        reduced.reshape(HALF_ROWS, 128),
        scratch=(pltpu.VMEM((8 * rank, 128), F32),) * 2,
    )
    theirs = lax.ppermute(mine, "row", swap)
    squares = lax.all_to_all(squares, ("row", "col"), 0, 0, axis_index_groups=plane)
    momentum_next, orthonormal = call(
        retain_kernel,
        (shape(mats, rows, cols), shape(mats, rows, 4 * rank, dtype=BF16)),
        here,
        mine,
        theirs,
        blended,
        projected,
        scalar=True,
        **work,
    )
    update, right = call(
        functools.partial(update_kernel, scale=scale),
        (shape(mats, rows, cols, dtype=BF16), shape(mats, rank, cols)),
        here,
        squares,
        mine,
        theirs,
        orthonormal,
        scalar=True,
    )
    return update, momentum_next, jnp.swapaxes(right, 1, 2)


def solution(mesh):
    return jax.shard_map(
        on_device,
        mesh=mesh,
        in_specs=(P(None, "row", "col"), P(None, "row", "col"), P(None, "col", None)),
        out_specs=(P(None, "row", "col"), P(None, "row", "col"), P(None, "col", None)),
        check_vma=False,
    )
```
